256 devices in a mesh: gx: 32 (over y, z_hi, core), gy: 8 (over z_lo, x).
Axes of the slice: x: 4, y: 4, z: 8 (z_hi: 4, z_lo: 2; z = z_hi * 2 + z_lo), core: 2. Of those that a mesh axis runs over, the one named last changes fastest.
Arguments:
- level_set: float32 [256, 64, 256], P('gx', 'gy'), may hold values from -6 to 6
- source: float32 [256, 64, 256], P('gx', 'gy'), may hold values from -8 to 8
- stiffness: float32 [256, 64, 256], P('gx', 'gy'), may hold values from 0.1 to 6
- snap_buffer: bfloat16 [8, 64, 16, 64], P(None, 'gx', 'gy'), may hold values from -4 to 4
- buffer_order: int32 [8], replicated, may hold values from 0 to 7, each once
- first_weight: bfloat16 [27, 64], replicated, may hold values from -1.25 to 1.25
- second_weight: bfloat16 [1728, 64], replicated, may hold values from -0.15625 to 0.15625
- out_grad: bfloat16 [8, 64, 16, 4096], P('gy', 'gx'), may hold values from -0.15625 to 0.15625
Outputs:
- new_level: float32 [256, 64, 256], P('gx', 'gy')
- pressure: float32 [256, 64, 256], P('gx', 'gy')
- dw_first: float32 [27, 64], replicated
- dw_second: float32 [1728, 64], replicated
The draws below stay inside these ranges and needn't reach their ends.
Inputs may be any that keep to these rules, and one draw needn't show every extreme that they name: buffer_order holds every slot of 0 to 7 once.
All inputs are finite; a program needn't handle non-finite values.
Results may differ from the reference program's by a relative error of at most 0.0035.
Values may be sent and summed in bfloat16 or wider, within the bound.
A program may use at most 64 MiB of HBM per device.

```python
import math
import jax
import jax.numpy as jnp
from jax import lax

FZ = 256
COARSEN = 4
CH = 64
ITERS = 20
NX = 256
NY = 64
CNX = 64
CNY = 16
CNZ = 64
SNAPS = 8


def shard_levels(key, extent, split, smallest, top_value):
    gain, own = 1.0, jax.random.fold_in(key, 6)
    for dim, shards_of in split:
        draws = jnp.exp(jax.random.uniform(jax.random.fold_in(own, dim), (shards_of,), jnp.float32, smallest / len(split), top_value / len(split)))
        gain = gain * jnp.repeat(draws, extent[dim] // shards_of).reshape([-1 if axis == dim else 1 for axis in range(len(extent))])
    return gain


def centred(own_key, extent, scale, limit, split=(), kind=jnp.bfloat16):
    array = scale * jax.random.normal(own_key, extent, jnp.float32)
    if split:
        array = array * shard_levels(own_key, extent, split, -0.22, 0.18)
    return jnp.clip(array, -limit, limit).astype(kind)


def setup_inputs(seed: int = 0) -> dict:
    splits = jax.random.split(jax.random.key(seed), 9)
    return {
        "level_set": centred(splits[0], (NX, NY, FZ), 1.0, 6.0, ((0, 32), (1, 8)), jnp.float32),
        "source": centred(splits[1], (NX, NY, FZ), 1.0, 8.0, ((0, 32), (1, 8)), jnp.float32),
        "stiffness": jnp.clip(jnp.exp(math.log(6.0) - 4.0943445 * jax.random.uniform(splits[2], (NX, NY, FZ), jnp.float32) ** shard_levels(splits[2], (NX, NY, FZ), ((0, 32), (1, 8)), -0.2, 0.2)), 0.1, 6.0),
        "snap_buffer": centred(splits[3], (SNAPS, CNX, CNY, CNZ), 0.3, 4.0, ((1, 32), (2, 8))),
        "buffer_order": jax.random.permutation(splits[4], SNAPS).astype(jnp.int32),
        "first_weight": centred(splits[5], (27, CH), 27 ** -0.5, 1.25),
        "second_weight": centred(splits[6], (27 * CH, CH), (27 * CH) ** -0.5, 0.15625),
        "out_grad": centred(splits[7], (SNAPS, CNX, CNY, CNZ * CH), (8 * (SNAPS * CNX * CNY * CNZ) ** -0.5), 0.15625, ((0, 8), (1, 32))),
    }


time_step = 2.0

def neighbours(padded):
    total = padded[2:, 1:-1, 1:-1] + padded[:-2, 1:-1, 1:-1]
    total = total + padded[1:-1, 2:, 1:-1] + padded[1:-1, :-2, 1:-1]
    return total + padded[1:-1, 1:-1, 2:] + padded[1:-1, 1:-1, :-2]

def advance(p_pad, f_pad, level):
    grad_px = 0.5 * (p_pad[2:, 1:-1, 1:-1] - p_pad[:-2, 1:-1, 1:-1])
    grad_py = 0.5 * (p_pad[1:-1, 2:, 1:-1] - p_pad[1:-1, :-2, 1:-1])
    grad_pz = 0.5 * (p_pad[1:-1, 1:-1, 2:] - p_pad[1:-1, 1:-1, :-2])
    grad_fx = 0.5 * (f_pad[2:, 1:-1, 1:-1] - f_pad[:-2, 1:-1, 1:-1])
    grad_fy = 0.5 * (f_pad[1:-1, 2:, 1:-1] - f_pad[1:-1, :-2, 1:-1])
    grad_fz = 0.5 * (f_pad[1:-1, 1:-1, 2:] - f_pad[1:-1, 1:-1, :-2])
    return level + time_step * (grad_px * grad_fx + grad_py * grad_fy + grad_pz * grad_fz)

def level_stack(padded, nx, ny, nz):
    rows = []
    for dx in range(3):
        for dy in range(3):
            for dz in range(3):
                rows.append(padded[:, dx:dx + nx, dy:dy + ny, dz:dz + nz].reshape(-1))
    return jnp.stack(rows, 0)

def first_layer(stack, weight):
    return lax.dot_general(stack, weight, (((0,), (0,)), ((), ())), preferred_element_type=jnp.float32)

def second_grad(h_pad, g_flat, nx, ny, nz):
    blocks = []
    for dx in range(3):
        for dy in range(3):
            block = jnp.concatenate([h_pad[:, dx:dx + nx, dy:dy + ny, dz:dz + nz, :] for dz in range(3)], axis=-1)
            block = block.reshape(-1, block.shape[-1])
            blocks.append(lax.dot_general(block, g_flat, (((0,), (0,)), ((), ())), preferred_element_type=jnp.float32))
    return jnp.concatenate(blocks, 0)

def back_features(g_pad, weight, nx, ny, nz):
    chans = g_pad.shape[-1]
    total = jnp.zeros((g_pad.shape[0] * nx * ny * nz, chans), jnp.float32)
    for dx in range(3):
        for dy in range(3):
            block = jnp.concatenate([g_pad[:, 2 - dx:2 - dx + nx, 2 - dy:2 - dy + ny, 2 - dz:2 - dz + nz, :] for dz in range(3)], axis=-1)
            block = block.reshape(-1, 3 * chans)
            mats = []
            for dz in range(3):
                off = dx * 9 + dy * 3 + dz
                mats.append(weight[off * chans:(off + 1) * chans, :].T)
            total = total + jnp.dot(block, jnp.concatenate(mats, 0), preferred_element_type=jnp.float32)
    return total

def silu_slope(z):
    sig = jax.nn.sigmoid(z)
    return sig * (1.0 + z * (1.0 - sig))

def reference(level_set, source, stiffness, snap_buffer, buffer_order, first_weight, second_weight, out_grad):

    def sweep(i, press):
        return (source + neighbours(jnp.pad(press, 1))) / (6.0 + stiffness)
    pressure = lax.fori_loop(0, ITERS, sweep, jnp.zeros_like(source))
    new_level = advance(jnp.pad(pressure, 1), jnp.pad(level_set, 1), level_set)
    coarse = new_level.reshape(CNX, COARSEN, CNY, COARSEN, CNZ, COARSEN).mean(axis=(1, 3, 5)).astype(jnp.bfloat16)
    chosen = (jnp.arange(SNAPS, dtype=jnp.int32) == buffer_order[0])[:, None, None, None]
    updated = jnp.where(chosen, coarse[None], snap_buffer)
    snaps = jnp.take(updated, buffer_order.astype(jnp.int32), axis=0)

    def one(carry, pair):
        snap, grad = pair
        a_pad = jnp.pad(snap[None], ((0, 0), (1, 1), (1, 1), (1, 1)))
        stack = level_stack(a_pad, CNX, CNY, CNZ)
        z_one = first_layer(stack, first_weight)
        h_one = jax.nn.silu(z_one).astype(jnp.bfloat16).reshape(1, CNX, CNY, CNZ, CH)
        h_pad = jnp.pad(h_one, ((0, 0), (1, 1), (1, 1), (1, 1), (0, 0)))
        g_five = grad.reshape(1, CNX, CNY, CNZ, CH)
        g_pad = jnp.pad(g_five, ((0, 0), (1, 1), (1, 1), (1, 1), (0, 0)))
        dw_two = second_grad(h_pad, g_five.reshape(-1, CH), CNX, CNY, CNZ)
        dh_one = back_features(g_pad, second_weight, CNX, CNY, CNZ)
        dz_one = (dh_one * silu_slope(z_one)).astype(jnp.bfloat16)
        dw_one = jnp.dot(stack, dz_one, preferred_element_type=jnp.float32)
        return ((carry[0] + dw_one, carry[1] + dw_two), None)
    init = (jnp.zeros((27, CH), jnp.float32), jnp.zeros((27 * CH, CH), jnp.float32))
    (dw_first, dw_second), _ = lax.scan(one, init, (snaps, out_grad))
    return (new_level, pressure, dw_first, dw_second)
```

```python
import functools

import jax
import jax.numpy as jnp
from jax import lax
from jax.experimental import pallas as pl
from jax.experimental.pallas import tpu as pltpu
from jax.sharding import PartitionSpec as P

F32 = jnp.float32
BF16 = jnp.bfloat16
MESH = pl.DeviceIdType.MESH
GX, GY = 32, 8
FZ = 256
T = 8
ROWS = 512
RAD = 6
GROUP = 32
CHUNKS = 28
ZS = 8
DIRS = [(dx, dy) for dx in (-1, 0, 1) for dy in (-1, 0, 1) if (dx, dy) != (0, 0)]


def dot(a, b, dims=((1,), (0,)), precision=None):
    return lax.dot_general(
        a, b, (dims, ((), ())), preferred_element_type=F32, precision=precision
    )


def iota(shape, dim):
    return lax.broadcasted_iota(jnp.int32, shape, dim)


def row_before(v):
    y = iota(v.shape, 0) & 15
    return jnp.where(y == 0, 0.0, pltpu.roll(v, 1, 0))


def row_after(v):
    y = iota(v.shape, 0) & 15
    return jnp.where(y == 15, 0.0, pltpu.roll(v, v.shape[0] - 1, 0))


def z_before(v, axis):
    z = iota(v.shape, axis)
    return jnp.where(z == 0, 0.0, pltpu.roll(v, 1, axis))


def z_after(v, axis):
    z = iota(v.shape, axis)
    return jnp.where(z == FZ - 1, 0.0, pltpu.roll(v, FZ - 1, axis))


def kernel(
    src, stf, lev, snp, order, w1, w2, g,
    newl, prs, dw1o, dw2o,
    A, B, PP, absend, abrcv, psend, prcv, fysend, fxr, fyr,
    snsend, snrcv, grcv, W, GT, BT, V, w1s, S6, CC, H3, DZ3, LT, dh, acc, d1,
    rsend, r1, r2, f3, r3,
    ab_ss, ab_rs, p_ss, p_rs, f_ss, f_rs, sn_ss, sn_rs, g_ss, g_rs,
    r1_ss, r1_rs, r2_ss, r2_rs, r3_ss, r3_rs,
):
    i = lax.axis_index("gx")
    j = lax.axis_index("gy")
    has_l, has_r = i > 0, i < GX - 1
    has_x = {-1: has_l, 0: True, 1: has_r}
    has_y = {-1: j > 0, 0: True, 1: j < GY - 1}

    def has(d):
        dx, dy = DIRS[d]
        if dx == 0:
            return has_y[dy]
        if dy == 0:
            return has_x[dx]
        return jnp.logical_and(has_x[dx], has_y[dy])

    cy, czh, cc = i // 8, (i // 2) % 4, i % 2
    czl, cx = j // 4, j % 4
    me = cy * 8 + cc * 4 + cx
    mez = czh * 2 + czl

    def member(m):
        return ((m // 8) * 8 + czh * 2 + (m // 4) % 2, czl * 4 + m % 4)

    def zpeer(k):
        return (cy * 8 + (k // 2) * 2 + cc, (k % 2) * 4 + cx)

    bar = pltpu.get_barrier_semaphore()

    def greet(dev):
        pl.semaphore_signal(bar, inc=1, device_id=dev, device_id_type=MESH)

    @pl.when(has_l)
    def _():
        @pl.loop(0, GY)
        def _(s):
            greet((i - 1, s))

    @pl.when(has_r)
    def _():
        @pl.loop(0, GY)
        def _(s):
            greet((i + 1, s))

    @pl.loop(1, GY)
    def _(k):
        greet((i, lax.rem(j + k, GY)))

    @pl.loop(1, GROUP)
    def _(k):
        greet(member(lax.rem(me + k, GROUP)))

    @pl.loop(1, ZS)
    def _(k):
        greet(zpeer(lax.rem(mez + k, ZS)))

    a_own = 1.0 / (6.0 + stf[...])
    b_own = src[...] * a_own
    A[8:16, 8:16, :] = a_own
    B[8:16, 8:16, :] = b_own
    PP[8:16, 8:16, :] = b_own
    absend[...] = jnp.concatenate([a_own, b_own], axis=1).astype(BF16)
    fysend[0] = lev[:, 0, :]
    fysend[1] = lev[:, 7, :]
    zero_tile = jnp.zeros((T, T, FZ), F32)
    for d, (dx, dy) in enumerate(DIRS):
        xs, ys = pl.ds(8 + 8 * dx, 8), pl.ds(8 + 8 * dy, 8)

        @pl.when(jnp.logical_not(has(d)))
        def _():
            A[xs, ys, :] = zero_tile
            B[xs, ys, :] = zero_tile
            PP[xs, ys, :] = zero_tile

    @pl.when(jnp.logical_not(has_l))
    def _():
        fxr[0] = jnp.zeros((T, FZ), F32)
        snrcv[0] = jnp.zeros((GY, 8, 128), F32)
        grcv[0] = jnp.zeros((16, 4096), BF16)

    @pl.when(jnp.logical_not(has_r))
    def _():
        fxr[1] = jnp.zeros((T, FZ), F32)
        snrcv[2] = jnp.zeros((GY, 8, 128), F32)
        grcv[1] = jnp.zeros((16, 4096), BF16)

    @pl.when(j == 0)
    def _():
        fyr[0] = jnp.zeros((T, FZ), F32)

    @pl.when(j == GY - 1)
    def _():
        fyr[1] = jnp.zeros((T, FZ), F32)

    for s in range(1, 8):
        snsend[s] = snp[order[s]]

    n_bar = (GY - 1) + (GROUP - 1) + (ZS - 1)
    n_bar = n_bar + jnp.where(has_l, GY, 0) + jnp.where(has_r, GY, 0)
    pl.semaphore_wait(bar, n_bar)

    def ab_copy(d, to):
        dx, dy = DIRS[d]
        slot = 7 - d if to else d
        send_dx = dx if to else -dx
        rows = {1: pl.ds(T - RAD, RAD), 0: pl.ds(0, T), -1: pl.ds(0, RAD)}[send_dx]
        return pltpu.make_async_remote_copy(
            src_ref=absend.at[rows], dst_ref=abrcv.at[slot, rows],
            send_sem=ab_ss.at[d], recv_sem=ab_rs.at[slot],
            device_id=(i + dx, j + dy), device_id_type=MESH,
        )

    def p_copy(e, d, to):
        dx, dy = DIRS[d]
        slot = 7 - d if to else d
        return pltpu.make_async_remote_copy(
            src_ref=psend.at[e], dst_ref=prcv.at[e, slot],
            send_sem=p_ss.at[e, d], recv_sem=p_rs.at[e, slot],
            device_id=(i + dx, j + dy), device_id_type=MESH,
        )

    def fx_copy(side, to):
        slot = 1 - side if to else side
        return pltpu.make_async_remote_copy(
            src_ref=lev.at[0 if side == 0 else 7], dst_ref=fxr.at[slot],
            send_sem=f_ss.at[side], recv_sem=f_rs.at[slot],
            device_id=(i + (2 * side - 1), j), device_id_type=MESH,
        )

    def fy_copy(side, to):
        slot = 1 - side if to else side
        return pltpu.make_async_remote_copy(
            src_ref=fysend.at[side], dst_ref=fyr.at[slot],
            send_sem=f_ss.at[2 + side], recv_sem=f_rs.at[2 + slot],
            device_id=(i, j + (2 * side - 1)), device_id_type=MESH,
        )

    def g_copy(side, to):
        slot = 1 - side if to else side
        return pltpu.make_async_remote_copy(
            src_ref=g.at[side], dst_ref=grcv.at[slot],
            send_sem=g_ss.at[side], recv_sem=g_rs.at[slot],
            device_id=(i + (2 * side - 1), j), device_id_type=MESH,
        )

    def sn_send(d, s):
        return pltpu.make_async_remote_copy(
            src_ref=snsend.at[s], dst_ref=snrcv.at[1 - d, j],
            send_sem=sn_ss.at[d + 1, s], recv_sem=sn_rs.at[1 - d, j],
            device_id=(i + d, s), device_id_type=MESH,
        )

    def sn_recv(d, y):
        return pltpu.make_async_remote_copy(
            src_ref=snsend.at[0], dst_ref=snrcv.at[d + 1, y],
            send_sem=sn_ss.at[d + 1, 0], recv_sem=sn_rs.at[d + 1, y],
            device_id=(i, j), device_id_type=MESH,
        )

    x_sides = ((0, has_l), (1, has_r))
    y_sides = ((0, has_y[-1]), (1, has_y[1]))

    for d in range(8):
        pl.when(has(d))(lambda d=d: ab_copy(d, True).start())
    for side, ok in x_sides:
        pl.when(ok)(lambda side=side: fx_copy(side, True).start())
    for side, ok in y_sides:
        pl.when(ok)(lambda side=side: fy_copy(side, True).start())
    for side, ok in x_sides:
        pl.when(ok)(lambda side=side: g_copy(side, True).start())

    def each_snap(lo, hi, act):
        @pl.loop(lo, hi)
        def _(s):
            pl.when(has_l)(lambda: act(-1, s))
            pl.when(s != j)(lambda: act(0, s))
            pl.when(has_r)(lambda: act(1, s))

    each_snap(1, GY, lambda d, s: sn_send(d, s).start())

    for a in range(3):
        for b in range(3):
            blk = [
                w2[(9 * a + 3 * b + c) * 64 : (9 * a + 3 * b + c + 1) * 64, :].astype(F32)
                for c in range(3)
            ]
            none = jnp.zeros((64, 64), F32)
            r0 = (b * 2) * 64
            BT[a, r0 : r0 + 64, :] = jnp.concatenate(
                [blk[2], blk[1], blk[0], none], axis=1
            ).astype(BF16)
            BT[a, r0 + 64 : r0 + 128, :] = jnp.concatenate(
                [none, blk[2], blk[1], blk[0]], axis=1
            ).astype(BF16)

    w1s[...] = jnp.zeros((32, 128), F32)
    w1s[0:27, 0:64] = w1[...].astype(F32)
    w1d = w1s[...]
    w1d = jnp.concatenate([w1d, pltpu.roll(w1d, 64, 1)], axis=0).astype(BF16)
    for par in range(2):
        for b in range(3):
            k = iota((256, 64), 0)
            col = iota((256, 64), 1)
            zo = col // 32
            zi = ((k & 63) + 5 - 2 * par) & 3
            cz = zi - zo
            want = 9 * (k // 64) + 3 * b + cz
            hit = (col % 32 == want) & (cz >= 0) & (cz < 3) & (k < 192)
            V[par, :, b * 128 : (b + 1) * 128] = dot(
                jnp.where(hit, 1.0, 0.0).astype(BF16), w1d
            ).astype(BF16)

    lane128 = iota((16, 128), 1)

    def windows(plane, gv):
        gr = pltpu.roll(gv.astype(F32), 64, 1)
        for t in range(33):
            if t == 0:
                tile = jnp.where(lane128 >= 64, gr[:, 0:128], 0.0)
            elif t == 32:
                tile = jnp.where(lane128 < 64, gr[:, 0:128], 0.0)
            else:
                tile = gr[:, 128 * t : 128 * (t + 1)]
            tile = tile.astype(BF16)
            if t < 32:
                r = ((t % 2) * 16 + t // 2) * 16
                W[plane, r : r + 16, 0:128] = tile
            if t > 0:
                r = (((t - 1) % 2) * 16 + (t - 1) // 2) * 16
                W[plane, r : r + 16, 128:256] = tile

    for x in range(2):
        windows(x + 1, g[x])
        GT[x] = W[x + 1].T

    for d, (dx, dy) in enumerate(DIRS):
        lo = {-1: T - RAD, 0: 0, 1: 0}[dx]
        n = T if dx == 0 else RAD
        xs, ys = pl.ds(8 + 8 * dx + lo, n), pl.ds(8 + 8 * dy, 8)

        @pl.when(has(d))
        def _():
            ab_copy(d, False).wait_recv()
            v = abrcv[d, lo : lo + n].astype(F32)
            A[xs, ys, :] = v[:, 0:8]
            B[xs, ys, :] = v[:, 8:16]
            PP[xs, ys, :] = v[:, 8:16]

    def around(v):
        rows = pltpu.roll(v, 1, 0) + pltpu.roll(v, 23, 0)
        return rows + z_before(v, 1) + z_after(v, 1)

    def sweeps(first, count):
        @pl.loop(0, count)
        def _(it):
            rad = first - it
            lo = 8 - rad

            def body(t, carry):
                before, cur = carry
                x = lo + 2 * t
                n1 = PP[x + 1]
                n2 = PP[x + 2]
                PP[x] = B[x] + A[x] * (before + n1 + around(cur))
                PP[x + 1] = B[x + 1] + A[x + 1] * (cur + n2 + around(n1))
                return n1, n2

            lax.fori_loop(0, 4 + rad, body, (PP[lo - 1], PP[lo]))

    def exchange(e, filler):
        own = PP[8:16, 8:16, :]
        psend[e] = own.reshape(4, 16, FZ).astype(BF16)
        for d in range(8):
            pl.when(has(d))(lambda d=d: p_copy(e, d, True).start())
        filler()
        for d, (dx, dy) in enumerate(DIRS):
            xs, ys = pl.ds(8 + 8 * dx, 8), pl.ds(8 + 8 * dy, 8)

            @pl.when(has(d))
            def _():
                p_copy(e, d, False).wait_recv()
                PP[xs, ys, :] = prcv[e, d].astype(F32).reshape(8, 8, FZ)

    def back(x):
        @pl.loop(0, 4)
        def _(q):
            rows = pl.ds(pl.multiple_of(q * 128, 128), 128)
            r = dot(W[x + 2, rows, :], BT[0], ((1,), (1,)))
            r = r + dot(W[x + 1, rows, :], BT[1], ((1,), (1,)))
            r = r + dot(W[x, rows, :], BT[2], ((1,), (1,)))
            dh[x, rows, :] = (
                row_after(r[:, 0:128]) + r[:, 128:256] + row_before(r[:, 256:384])
            )

    def filler_one():
        for side, ok in x_sides:
            pl.when(ok)(lambda side=side: g_copy(side, False).wait_recv())
        windows(0, grcv[0])
        windows(3, grcv[1])
        back(0)

    def filler_two():
        back(1)

    sweeps(RAD - 1, RAD)
    exchange(0, filler_one)
    sweeps(6, 7)
    exchange(1, filler_two)
    sweeps(6, 6)

    for side, ok in x_sides:
        pl.when(ok)(lambda side=side: fx_copy(side, False).wait_recv())
    for side, ok in y_sides:
        pl.when(ok)(lambda side=side: fy_copy(side, False).wait_recv())

    pool = jnp.where(iota((FZ, 128), 0) // 4 == iota((FZ, 128), 1), 1.0 / 64.0, 0.0)
    row8 = iota((8, FZ), 0)
    sums = []
    total = None
    for x in range(8):
        pc = PP[x + 8]
        px = 0.5 * (PP[x + 9, 8:16] - PP[x + 7, 8:16])
        py = 0.5 * (pltpu.roll(pc, 23, 0) - pltpu.roll(pc, 1, 0))[8:16]
        pm = pc[8:16]
        pz = 0.5 * (z_after(pm, 1) - z_before(pm, 1))
        fm = lev[x]
        f_lo = fxr[0] if x == 0 else lev[x - 1]
        f_hi = fxr[1] if x == 7 else lev[x + 1]
        fx = 0.5 * (f_hi - f_lo)
        y_lo = jnp.where(row8 == 0, fyr[0, x : x + 1, :], pltpu.roll(fm, 1, 0))
        y_hi = jnp.where(row8 == 7, fyr[1, x : x + 1, :], pltpu.roll(fm, 7, 0))
        fy = 0.5 * (y_hi - y_lo)
        fz = 0.5 * (z_after(fm, 1) - z_before(fm, 1))
        new = fm + 2.0 * (px * fx + py * fy + pz * fz)
        newl[x] = new
        prs[x] = pm
        total = new if x % 4 == 0 else total + new
        if x % 4 == 3:
            t = total + pltpu.roll(total, 7, 0)
            sums.append(t + pltpu.roll(t, 6, 0))
    mean = dot(jnp.concatenate(sums, axis=0), pool, precision=lax.Precision.HIGHEST)
    for r in range(4):
        snsend[0, r : r + 1, :] = mean[4 * r : 4 * r + 1, :]
    snsend[0, 4:8, :] = jnp.zeros((4, 128), F32)

    each_snap(0, 1, lambda d, s: sn_send(d, s).start())
    snrcv[1, j] = snsend[j]

    @pl.when(has_l)
    def _():
        @pl.loop(0, GY)
        def _(y):
            sn_recv(-1, y).wait_recv()

    @pl.when(has_r)
    def _():
        @pl.loop(0, GY)
        def _(y):
            sn_recv(1, y).wait_recv()

    @pl.loop(1, GY)
    def _(k):
        sn_recv(0, lax.rem(j + k, GY)).wait_recv()

    for d in range(3):
        for y in range(8):
            t = snrcv[d, y]
            S6[2 * d, 2 * y : 2 * y + 2, :] = t[0:2]
            S6[2 * d + 1, 2 * y : 2 * y + 2, :] = t[2:4]
    for p in range(4):
        CC[p, :, 0:128] = S6[p] + pltpu.roll(S6[p + 1], 64, 1)
        CC[p, :, 128:256] = S6[p + 2]

    for p in range(4):
        keep = {0: jnp.where(has_l, 1.0, 0.0), 3: jnp.where(has_r, 1.0, 0.0)}.get(p)

        @pl.loop(0, 4)
        def _(q):
            rows = pl.ds(pl.multiple_of(q * 128, 128), 128)
            par = q // 2
            jj = 2 * ((q % 2) * 8 + iota((8, 16, 256), 0)) + par
            t = (iota((8, 16, 256), 2) & 63) - 2 * jj + 1
            mask = (t >= 0) & (t < 4)
            v = jnp.broadcast_to(CC[p][None], (8, 16, 256))
            v = jnp.where(mask, v, 0.0).reshape(128, 256).astype(BF16)
            r = dot(v, V[par])
            z = row_before(r[:, 0:128]) + r[:, 128:256] + row_after(r[:, 256:384])
            sig = 1.0 / (1.0 + jnp.exp(-z))
            h = z * sig
            if keep is not None:
                h = h * keep
            H3[p, rows, 0:128] = row_before(h).astype(BF16)
            H3[p, rows, 128:256] = h.astype(BF16)
            H3[p, rows, 256:384] = row_after(h).astype(BF16)
            if p in (1, 2):
                dz = dh[p - 1, rows, :] * (sig * (1.0 + z * (1.0 - sig)))
                DZ3[p - 1, rows, 0:128] = row_after(dz).astype(BF16)
                DZ3[p - 1, rows, 128:256] = dz.astype(BF16)
                DZ3[p - 1, rows, 256:384] = row_before(dz).astype(BF16)

    for a in range(3):
        acc[a] = dot(GT[0], H3[a]) + dot(GT[1], H3[a + 1])

    spread = jnp.where((iota((16, ROWS), 1) & 15) == iota((16, ROWS), 0), 1.0, 0.0).astype(BF16)
    r_k = iota((256, ROWS), 0) & 63
    r_c = iota((256, ROWS), 1)
    jj = 2 * ((r_c & 255) // 16) + r_c // 256
    t = r_k - 2 * jj + 1
    near = (t >= 0) & (t < 4)
    for x in range(2):
        LT[x] = jnp.where(near, dot(CC[x + 1].T.astype(BF16), spread), 0.0).astype(BF16)
    parts = []
    for par in range(2):
        cols = slice(par * 256, par * 256 + 256)
        q = dot(LT[0, :, cols], DZ3[0, cols, :]) + dot(LT[1, :, cols], DZ3[1, cols, :])
        q = q.reshape(4, 8, 8, 384)
        parts.append([q[a].sum(0) for a in range(3)])
    d1[...] = jnp.zeros((64, 128), F32)
    for a in range(3):
        u, w = parts[0][a], parts[1][a]
        u = u + pltpu.roll(u, 4, 0)
        w = w + pltpu.roll(w, 4, 0)
        u = u + pltpu.roll(w, 2, 0)
        for b in range(3):
            v = u[:, b * 128 : (b + 1) * 128]
            v = pltpu.roll(v, 64, 1) + pltpu.roll(v, 7, 0)
            v = pltpu.roll(v, 1, 0)
            d1[9 * a + 3 * b : 9 * a + 3 * b + 3, :] = v[0:3]

    lane = iota((64, 128), 1)

    def term(o):
        a, b, c = o // 9, (o // 3) % 3, o % 3
        r = (2 - c) * 64
        cols = slice(b * 128, b * 128 + 128)
        v = jnp.where(lane < 64, acc[a, r : r + 64, cols], acc[a, r + 64 : r + 128, cols])
        return v + pltpu.roll(v, 64, 1)

    for q in range(14):
        other = term(2 * q + 1) if q < 13 else d1[...]
        v = jnp.where(lane < 64, term(2 * q), other)
        rsend[2 * q] = v[0:32].astype(BF16)
        rsend[2 * q + 1] = v[32:64].astype(BF16)

    def r1_send(m):
        return pltpu.make_async_remote_copy(
            src_ref=rsend.at[m], dst_ref=r1.at[me],
            send_sem=r1_ss.at[m], recv_sem=r1_rs.at[me],
            device_id=member(m), device_id_type=MESH,
        )

    def r1_recv(m):
        return pltpu.make_async_remote_copy(
            src_ref=rsend.at[0], dst_ref=r1.at[m],
            send_sem=r1_ss.at[0], recv_sem=r1_rs.at[m],
            device_id=member(m), device_id_type=MESH,
        )

    def r2_copy(k, slot):
        return pltpu.make_async_remote_copy(
            src_ref=r2.at[mez], dst_ref=r2.at[slot],
            send_sem=r2_ss.at[k], recv_sem=r2_rs.at[slot],
            device_id=zpeer(k), device_id_type=MESH,
        )

    def r3_copy(m, slot):
        return pltpu.make_async_remote_copy(
            src_ref=f3, dst_ref=r3.at[slot],
            send_sem=r3_ss.at[m], recv_sem=r3_rs.at[slot],
            device_id=member(m), device_id_type=MESH,
        )

    @pl.loop(1, GROUP)
    def _(k):
        m = lax.rem(me + k, GROUP)
        pl.when(m < CHUNKS)(lambda: r1_send(m).start())

    @pl.when(me < CHUNKS)
    def _():
        def add(k, total):
            m = lax.rem(me + k, GROUP)
            r1_recv(m).wait_recv()
            return total + r1[m].astype(F32)

        r2[mez] = lax.fori_loop(1, GROUP, add, rsend[me].astype(F32))

        @pl.loop(1, ZS)
        def _(k):
            r2_copy(lax.rem(mez + k, ZS), mez).start()

        @pl.loop(1, ZS)
        def _(k):
            m = lax.rem(mez + k, ZS)
            r2_copy(m, m).wait_recv()

        total = r2[0]
        for k in range(1, ZS):
            total = total + r2[k]
        f3[...] = total.astype(BF16)

        @pl.loop(1, GROUP)
        def _(k):
            r3_copy(lax.rem(me + k, GROUP), me).start()

        r3[me] = f3[...]

    @pl.loop(1, GROUP)
    def _(k):
        m = lax.rem(me + k, GROUP)
        pl.when(m < CHUNKS)(lambda: r3_copy(m, m).wait_recv())

    for q in range(14):
        v = jnp.concatenate([r3[2 * q], r3[2 * q + 1]], axis=0).astype(F32)
        vt = v.T
        if q < 13:
            dw2o[128 * q : 128 * q + 128, :] = vt
        else:
            dw2o[128 * q : 128 * q + 64, :] = vt[0:64]
            dw1o[...] = pltpu.roll(v, 64, 1)[0:27, 0:64]

    for d in range(8):
        @pl.when(has(d))
        def _():
            ab_copy(d, True).wait_send()
            p_copy(0, d, True).wait_send()
            p_copy(1, d, True).wait_send()

    for side, ok in x_sides:
        @pl.when(ok)
        def _():
            fx_copy(side, True).wait_send()
            g_copy(side, True).wait_send()

    for side, ok in y_sides:
        pl.when(ok)(lambda side=side: fy_copy(side, True).wait_send())
    each_snap(0, GY, lambda d, s: sn_send(d, s).wait_send())

    @pl.loop(1, GROUP)
    def _(k):
        m = lax.rem(me + k, GROUP)
        pl.when(m < CHUNKS)(lambda: r1_send(m).wait_send())
        pl.when(me < CHUNKS)(lambda: r3_copy(m, me).wait_send())

    @pl.when(me < CHUNKS)
    def _():
        @pl.loop(1, ZS)
        def _(k):
            r2_copy(lax.rem(mez + k, ZS), mez).wait_send()


def per_device(
    level_set, source, stiffness, snap_buffer, buffer_order, first_weight, second_weight, out_grad
):
    snap = jnp.pad(
        snap_buffer.reshape(8, 4, 64).astype(F32), ((0, 0), (0, 4), (0, 64))
    )
    g = out_grad.reshape(2, 16, 4096)
    vm = pl.BlockSpec(memory_space=pltpu.VMEM)
    sm = pl.BlockSpec(memory_space=pltpu.SMEM)
    dma = pltpu.SemaphoreType.DMA
    return pl.pallas_call(
        kernel,
        out_shape=(
            jax.ShapeDtypeStruct((8, 8, FZ), F32),
            jax.ShapeDtypeStruct((8, 8, FZ), F32),
            jax.ShapeDtypeStruct((27, 64), F32),
            jax.ShapeDtypeStruct((1728, 64), F32),
        ),
        in_specs=[vm, vm, vm, vm, sm, vm, vm, vm],
        out_specs=(vm, vm, vm, vm),
        scratch_shapes=[
            pltpu.VMEM((24, 24, FZ), F32),
            pltpu.VMEM((24, 24, FZ), F32),
            pltpu.VMEM((24, 24, FZ), F32),
            pltpu.VMEM((8, 16, FZ), BF16),
            pltpu.VMEM((8, 8, 16, FZ), BF16),
            pltpu.VMEM((2, 4, 16, FZ), BF16),
            pltpu.VMEM((2, 8, 4, 16, FZ), BF16),
            pltpu.VMEM((2, 8, FZ), F32),
            pltpu.VMEM((2, 8, FZ), F32),
            pltpu.VMEM((2, 8, FZ), F32),
            pltpu.VMEM((8, 8, 128), F32),
            pltpu.VMEM((3, 8, 8, 128), F32),
            pltpu.VMEM((2, 16, 4096), BF16),
            pltpu.VMEM((4, ROWS, 256), BF16),
            pltpu.VMEM((2, 256, ROWS), BF16),
            pltpu.VMEM((3, 384, 256), BF16),
            pltpu.VMEM((2, 256, 384), BF16),
            pltpu.VMEM((32, 128), F32),
            pltpu.VMEM((6, 16, 128), F32),
            pltpu.VMEM((4, 16, 256), F32),
            pltpu.VMEM((4, ROWS, 384), BF16),
            pltpu.VMEM((2, ROWS, 384), BF16),
            pltpu.VMEM((2, 256, ROWS), BF16),
            pltpu.VMEM((2, ROWS, 128), F32),
            pltpu.VMEM((3, 256, 384), F32),
            pltpu.VMEM((64, 128), F32),
            pltpu.VMEM((CHUNKS, 32, 128), BF16),
            pltpu.VMEM((GROUP, 32, 128), BF16),
            pltpu.VMEM((ZS, 32, 128), F32),
            pltpu.VMEM((32, 128), BF16),
            pltpu.VMEM((CHUNKS, 32, 128), BF16),
            dma((8,)), dma((8,)), dma((2, 8)), dma((2, 8)), dma((4,)), dma((4,)),
            dma((3, 8)), dma((3, 8)), dma((2,)), dma((2,)),
            dma((CHUNKS,)), dma((GROUP,)), dma((ZS,)), dma((ZS,)), dma((GROUP,)), dma((CHUNKS,)),
        ],
        compiler_params=pltpu.CompilerParams(
            collective_id=0, has_side_effects=True, vmem_limit_bytes=48 * 1024 * 1024
        ),
    )(source, stiffness, level_set, snap, buffer_order, first_weight, second_weight, g)


def solution(mesh):
    placed = (
        P("gx", "gy", None),
        P("gx", "gy", None),
        P("gx", "gy", None),
        P(None, "gx", "gy", None),
        P(),
        P(),
        P(),
        P("gy", "gx", None, None),
    )
    return jax.shard_map(
        per_device,
        mesh=mesh,
        in_specs=placed,
        out_specs=(P("gx", "gy", None), P("gx", "gy", None), P(), P()),
        check_vma=False,
    )
```

```python
import functools

import jax
import jax.numpy as jnp
from jax import lax
from jax.experimental import pallas as pl
from jax.experimental.pallas import tpu as pltpu
from jax.sharding import PartitionSpec as P

F32 = jnp.float32
BF16 = jnp.bfloat16
MESH = pl.DeviceIdType.MESH
GX, GY = 32, 8
FZ = 256
T = 8
ROWS = 512
RAD = 6
GROUP = 32
CHUNKS = 28
ZS = 8
DIRS = [(dx, dy) for dx in (-1, 0, 1) for dy in (-1, 0, 1) if (dx, dy) != (0, 0)]


def dot(a, b, dims=((1,), (0,)), precision=None):
    return lax.dot_general(
        a, b, (dims, ((), ())), preferred_element_type=F32, precision=precision
    )


def iota(shape, dim):
    return lax.broadcasted_iota(jnp.int32, shape, dim)


def tile_rows(dx, n):
    return {-1: (T - n, n), 0: (0, T), 1: (0, n)}[dx]


def row_before(v):
    y = iota(v.shape, 0) & 15
    return jnp.where(y == 0, 0.0, pltpu.roll(v, 1, 0))


def row_after(v):
    y = iota(v.shape, 0) & 15
    return jnp.where(y == 15, 0.0, pltpu.roll(v, v.shape[0] - 1, 0))


def z_before(v, axis):
    z = iota(v.shape, axis)
    return jnp.where(z == 0, 0.0, pltpu.roll(v, 1, axis))


def z_after(v, axis):
    z = iota(v.shape, axis)
    return jnp.where(z == FZ - 1, 0.0, pltpu.roll(v, FZ - 1, axis))


def kernel(
    src_h, stf_h, lev_h, snp, order, w1, w2_h, g_h,
    newl_h, prs_h, dw1_h, dw2_h,
    newl, prs, dw1o, dw2o, out_s,
    src, stf, lev, w2, g, w2p, in_s,
    A, B, PP, absend, abrcv, psend, prcv, fysend, fxr, fyr,
    snsend, snrcv, grcv, W, GT, BT, V, w1s, S6, CC, H3, DZ3, LT, dh, acc, d1,
    rsend, r1, r2, f3, r3,
    ab_ss, ab_rs, p_ss, p_rs, f_ss, f_rs, sn_ss, sn_rs, g_ss, g_rs,
    r1_ss, r1_rs, r2_ss, r2_rs, r3_ss, r3_rs,
):
    i = lax.axis_index("gx")
    j = lax.axis_index("gy")
    has_l, has_r = i > 0, i < GX - 1
    has_x = {-1: has_l, 0: True, 1: has_r}
    has_y = {-1: j > 0, 0: True, 1: j < GY - 1}

    def has(d):
        dx, dy = DIRS[d]
        if dx == 0:
            return has_y[dy]
        if dy == 0:
            return has_x[dx]
        return jnp.logical_and(has_x[dx], has_y[dy])

    cy, czh, cc = i // 8, (i // 2) % 4, i % 2
    czl, cx = j // 4, j % 4
    me = cy * 8 + cc * 4 + cx
    mez = czh * 2 + czl

    def member(m):
        return ((m // 8) * 8 + czh * 2 + (m // 4) % 2, czl * 4 + m % 4)

    def zpeer(k):
        return (cy * 8 + (k // 2) * 2 + cc, (k % 2) * 4 + cx)

    loads = [
        pltpu.make_async_copy(a, b, in_s.at[k])
        for k, (a, b) in enumerate(
            ((src_h, src), (stf_h, stf), (lev_h, lev), (g_h, g), (w2_h, w2))
        )
    ]
    for c in loads:
        c.start()

    bar = pltpu.get_barrier_semaphore()

    def greet(dev):
        pl.semaphore_signal(bar, inc=1, device_id=dev, device_id_type=MESH)

    @pl.when(has_l)
    def _():
        @pl.loop(0, GY)
        def _(s):
            greet((i - 1, s))

    @pl.when(has_r)
    def _():
        @pl.loop(0, GY)
        def _(s):
            greet((i + 1, s))

    @pl.loop(1, GY)
    def _(k):
        greet((i, lax.rem(j + k, GY)))

    @pl.loop(1, GROUP)
    def _(k):
        greet(member(lax.rem(me + k, GROUP)))

    @pl.loop(1, ZS)
    def _(k):
        greet(zpeer(lax.rem(mez + k, ZS)))

    for c in loads[:4]:
        c.wait()
    a_own = 1.0 / (6.0 + stf[...])
    b_own = src[...] * a_own
    A[8:16, 8:16, :] = a_own
    B[8:16, 8:16, :] = b_own
    PP[8:16, 8:16, :] = b_own
    absend[...] = jnp.concatenate([a_own, b_own], axis=1).astype(BF16)
    fysend[0] = lev[:, 0, :]
    fysend[1] = lev[:, 7, :]
    zero_tile = jnp.zeros((T, T, FZ), F32)
    for d, (dx, dy) in enumerate(DIRS):
        xs, ys = pl.ds(8 + 8 * dx, 8), pl.ds(8 + 8 * dy, 8)

        @pl.when(jnp.logical_not(has(d)))
        def _():
            A[xs, ys, :] = zero_tile
            B[xs, ys, :] = zero_tile
            PP[xs, ys, :] = zero_tile

    @pl.when(jnp.logical_not(has_l))
    def _():
        fxr[0] = jnp.zeros((T, FZ), F32)
        snrcv[0] = jnp.zeros((GY, 8, 128), F32)
        grcv[0] = jnp.zeros((16, 4096), BF16)

    @pl.when(jnp.logical_not(has_r))
    def _():
        fxr[1] = jnp.zeros((T, FZ), F32)
        snrcv[2] = jnp.zeros((GY, 8, 128), F32)
        grcv[1] = jnp.zeros((16, 4096), BF16)

    @pl.when(j == 0)
    def _():
        fyr[0] = jnp.zeros((T, FZ), F32)

    @pl.when(j == GY - 1)
    def _():
        fyr[1] = jnp.zeros((T, FZ), F32)

    snsend[...] = jnp.zeros((8, 8, 128), F32)
    for s in range(1, 8):
        snsend[s, 0:4, 0:64] = snp[order[s]].astype(F32)

    n_bar = (GY - 1) + (GROUP - 1) + (ZS - 1)
    n_bar = n_bar + jnp.where(has_l, GY, 0) + jnp.where(has_r, GY, 0)
    pl.semaphore_wait(bar, n_bar)

    def ab_copy(d, to):
        dx, dy = DIRS[d]
        slot = 7 - d if to else d
        send_dx = dx if to else -dx
        lo, n = tile_rows(-send_dx, RAD if dy == 0 else RAD - 1)
        rows = pl.ds(lo, n)
        return pltpu.make_async_remote_copy(
            src_ref=absend.at[rows], dst_ref=abrcv.at[slot, rows],
            send_sem=ab_ss.at[d], recv_sem=ab_rs.at[slot],
            device_id=(i + dx, j + dy), device_id_type=MESH,
        )

    def p_copy(e, d, to):
        dx, dy = DIRS[d]
        slot = 7 - d if to else d
        lo, n = tile_rows(-dx if to else dx, 8 if dy == 0 else 6)
        rows = pl.ds(lo // 2, n // 2)
        return pltpu.make_async_remote_copy(
            src_ref=psend.at[e, rows], dst_ref=prcv.at[e, slot, rows],
            send_sem=p_ss.at[e, d], recv_sem=p_rs.at[e, slot],
            device_id=(i + dx, j + dy), device_id_type=MESH,
        )

    def fx_copy(side, to):
        slot = 1 - side if to else side
        return pltpu.make_async_remote_copy(
            src_ref=lev.at[0 if side == 0 else 7], dst_ref=fxr.at[slot],
            send_sem=f_ss.at[side], recv_sem=f_rs.at[slot],
            device_id=(i + (2 * side - 1), j), device_id_type=MESH,
        )

    def fy_copy(side, to):
        slot = 1 - side if to else side
        return pltpu.make_async_remote_copy(
            src_ref=fysend.at[side], dst_ref=fyr.at[slot],
            send_sem=f_ss.at[2 + side], recv_sem=f_rs.at[2 + slot],
            device_id=(i, j + (2 * side - 1)), device_id_type=MESH,
        )

    def g_copy(side, to):
        slot = 1 - side if to else side
        return pltpu.make_async_remote_copy(
            src_ref=g.at[side], dst_ref=grcv.at[slot],
            send_sem=g_ss.at[side], recv_sem=g_rs.at[slot],
            device_id=(i + (2 * side - 1), j), device_id_type=MESH,
        )

    def sn_send(d, s):
        return pltpu.make_async_remote_copy(
            src_ref=snsend.at[s], dst_ref=snrcv.at[1 - d, j],
            send_sem=sn_ss.at[d + 1, s], recv_sem=sn_rs.at[1 - d, j],
            device_id=(i + d, s), device_id_type=MESH,
        )

    def sn_recv(d, y):
        return pltpu.make_async_remote_copy(
            src_ref=snsend.at[0], dst_ref=snrcv.at[d + 1, y],
            send_sem=sn_ss.at[d + 1, 0], recv_sem=sn_rs.at[d + 1, y],
            device_id=(i, j), device_id_type=MESH,
        )

    x_sides = ((0, has_l), (1, has_r))
    y_sides = ((0, has_y[-1]), (1, has_y[1]))

    for d in range(8):
        pl.when(has(d))(lambda d=d: ab_copy(d, True).start())
    for side, ok in x_sides:
        pl.when(ok)(lambda side=side: fx_copy(side, True).start())
    for side, ok in y_sides:
        pl.when(ok)(lambda side=side: fy_copy(side, True).start())
    for side, ok in x_sides:
        pl.when(ok)(lambda side=side: g_copy(side, True).start())

    def each_snap(lo, hi, act):
        @pl.loop(lo, hi)
        def _(s):
            pl.when(has_l)(lambda: act(-1, s))
            pl.when(s != j)(lambda: act(0, s))
            pl.when(has_r)(lambda: act(1, s))

    each_snap(1, GY, lambda d, s: sn_send(d, s).start())

    loads[4].wait()
    w2p[:, 0:1728] = w2[...].astype(F32)
    even = w2p[...]
    odd = pltpu.roll(even, 64, 1)
    left = iota((64, 128), 1) < 64

    def pair(o):
        t = ((o + 1) // 2) * 128
        return (odd if o % 2 else even)[:, t : t + 128]

    for a in range(3):
        for b in range(3):
            o = 9 * a + 3 * b
            tiles = (
                jnp.where(left, pair(o + 2), 0.0),
                pair(o + 1),
                pair(o),
                jnp.where(left, 0.0, pair(o - 1)),
            )
            for k, v in enumerate(tiles):
                BT[a, 64 * k : 64 * k + 64, 128 * b : 128 * b + 128] = v.astype(BF16)

    w1s[...] = jnp.zeros((32, 128), F32)
    w1s[0:27, 0:64] = w1[...].astype(F32)
    w1d = w1s[...]
    w1d = jnp.concatenate([w1d, pltpu.roll(w1d, 64, 1)], axis=0).astype(BF16)
    for par in range(2):
        for b in range(3):
            k = iota((256, 64), 0)
            col = iota((256, 64), 1)
            zo = col // 32
            zi = ((k & 63) + 5 - 2 * par) & 3
            cz = zi - zo
            want = 9 * (k // 64) + 3 * b + cz
            hit = (col % 32 == want) & (cz >= 0) & (cz < 3) & (k < 192)
            V[par, :, b * 128 : (b + 1) * 128] = dot(
                jnp.where(hit, 1.0, 0.0).astype(BF16), w1d
            ).astype(BF16)

    lane128 = iota((16, 128), 1)

    def windows(plane, gv):
        gr = pltpu.roll(gv.astype(F32), 64, 1)
        for t in range(33):
            if t == 0:
                tile = jnp.where(lane128 >= 64, gr[:, 0:128], 0.0)
            elif t == 32:
                tile = jnp.where(lane128 < 64, gr[:, 0:128], 0.0)
            else:
                tile = gr[:, 128 * t : 128 * (t + 1)]
            tile = tile.astype(BF16)
            if t < 32:
                r = ((t % 2) * 16 + t // 2) * 16
                W[plane, r : r + 16, 0:128] = tile
            if t > 0:
                r = (((t - 1) % 2) * 16 + (t - 1) // 2) * 16
                W[plane, r : r + 16, 128:256] = tile

    for x in range(2):
        windows(x + 1, g[x])
        GT[x] = W[x + 1].T

    for d, (dx, dy) in enumerate(DIRS):
        lo, n = tile_rows(dx, RAD if dy == 0 else RAD - 1)
        xs, ys = pl.ds(8 + 8 * dx + lo, n), pl.ds(8 + 8 * dy, 8)

        @pl.when(has(d))
        def _():
            ab_copy(d, False).wait_recv()
            v = abrcv[d, lo : lo + n].astype(F32)
            A[xs, ys, :] = v[:, 0:8]
            B[xs, ys, :] = v[:, 8:16]
            PP[xs, ys, :] = v[:, 8:16]

    def around(v):
        rows = pltpu.roll(v, 1, 0) + pltpu.roll(v, 23, 0)
        return rows + z_before(v, 1) + z_after(v, 1)

    def sweeps(first, count):
        for rad in range(first, first - count, -1):
            lo, hi = 8 - rad, 16 + rad
            before, cur = PP[lo - 1], PP[lo]
            for x in range(lo, hi):
                after = PP[x + 1]
                PP[x] = B[x] + A[x] * (before + after + around(cur))
                before, cur = cur, after

    def exchange(e, filler):
        own = PP[8:16, 8:16, :]
        psend[e] = own.reshape(4, 16, FZ).astype(BF16)
        for d in range(8):
            pl.when(has(d))(lambda d=d: p_copy(e, d, True).start())
        filler()
        for d, (dx, dy) in enumerate(DIRS):
            lo, n = tile_rows(dx, 8 if dy == 0 else 6)
            xs, ys = pl.ds(8 + 8 * dx + lo, n), pl.ds(8 + 8 * dy, 8)

            @pl.when(has(d))
            def _():
                p_copy(e, d, False).wait_recv()
                v = prcv[e, d, lo // 2 : (lo + n) // 2].astype(F32)
                PP[xs, ys, :] = v.reshape(n, 8, FZ)

    def back(x):
        @pl.loop(0, 4)
        def _(q):
            rows = pl.ds(pl.multiple_of(q * 128, 128), 128)
            r = dot(W[x + 2, rows, :], BT[0])
            r = r + dot(W[x + 1, rows, :], BT[1])
            r = r + dot(W[x, rows, :], BT[2])
            dh[x, rows, :] = (
                row_after(r[:, 0:128]) + r[:, 128:256] + row_before(r[:, 256:384])
            )

    def filler_one():
        for side, ok in x_sides:
            pl.when(ok)(lambda side=side: g_copy(side, False).wait_recv())
        windows(0, grcv[0])
        windows(3, grcv[1])
        back(0)

    def filler_two():
        back(1)

    sweeps(RAD - 1, RAD)
    exchange(0, filler_one)
    sweeps(6, 7)
    exchange(1, filler_two)
    sweeps(6, 6)

    for side, ok in x_sides:
        pl.when(ok)(lambda side=side: fx_copy(side, False).wait_recv())
    for side, ok in y_sides:
        pl.when(ok)(lambda side=side: fy_copy(side, False).wait_recv())

    pool = jnp.where(iota((FZ, 128), 0) // 4 == iota((FZ, 128), 1), 1.0 / 64.0, 0.0)
    row8 = iota((8, FZ), 0)
    sums = []
    total = None
    for x in range(8):
        pc = PP[x + 8]
        px = 0.5 * (PP[x + 9, 8:16] - PP[x + 7, 8:16])
        py = 0.5 * (pltpu.roll(pc, 23, 0) - pltpu.roll(pc, 1, 0))[8:16]
        pm = pc[8:16]
        pz = 0.5 * (z_after(pm, 1) - z_before(pm, 1))
        fm = lev[x]
        f_lo = fxr[0] if x == 0 else lev[x - 1]
        f_hi = fxr[1] if x == 7 else lev[x + 1]
        fx = 0.5 * (f_hi - f_lo)
        y_lo = jnp.where(row8 == 0, fyr[0, x : x + 1, :], pltpu.roll(fm, 1, 0))
        y_hi = jnp.where(row8 == 7, fyr[1, x : x + 1, :], pltpu.roll(fm, 7, 0))
        fy = 0.5 * (y_hi - y_lo)
        fz = 0.5 * (z_after(fm, 1) - z_before(fm, 1))
        new = fm + 2.0 * (px * fx + py * fy + pz * fz)
        newl[x] = new
        prs[x] = pm
        total = new if x % 4 == 0 else total + new
        if x % 4 == 3:
            t = total + pltpu.roll(total, 7, 0)
            sums.append(t + pltpu.roll(t, 6, 0))
    mean = dot(jnp.concatenate(sums, axis=0), pool, precision=lax.Precision.HIGHEST)
    for r in range(4):
        snsend[0, r : r + 1, :] = mean[4 * r : 4 * r + 1, :]
    snsend[0, 4:8, :] = jnp.zeros((4, 128), F32)

    each_snap(0, 1, lambda d, s: sn_send(d, s).start())
    stores = [
        pltpu.make_async_copy(a, b, out_s.at[k])
        for k, (a, b) in enumerate(
            ((newl, newl_h), (prs, prs_h), (dw1o, dw1_h), (dw2o, dw2_h))
        )
    ]
    stores[0].start()
    stores[1].start()
    snrcv[1, j] = snsend[j]

    @pl.when(has_l)
    def _():
        @pl.loop(0, GY)
        def _(y):
            sn_recv(-1, y).wait_recv()

    @pl.when(has_r)
    def _():
        @pl.loop(0, GY)
        def _(y):
            sn_recv(1, y).wait_recv()

    @pl.loop(1, GY)
    def _(k):
        sn_recv(0, lax.rem(j + k, GY)).wait_recv()

    for d in range(3):
        for y in range(8):
            t = snrcv[d, y]
            S6[2 * d, 2 * y : 2 * y + 2, :] = t[0:2]
            S6[2 * d + 1, 2 * y : 2 * y + 2, :] = t[2:4]
    for p in range(4):
        CC[p, :, 0:128] = S6[p] + pltpu.roll(S6[p + 1], 64, 1)
        CC[p, :, 128:256] = S6[p + 2]

    for p in range(4):
        keep = {0: jnp.where(has_l, 1.0, 0.0), 3: jnp.where(has_r, 1.0, 0.0)}.get(p)

        for q in range(4):
            rows = slice(q * 128, q * 128 + 128)
            par = q // 2
            jj = 2 * ((q % 2) * 8 + iota((8, 16, 256), 0)) + par
            t = (iota((8, 16, 256), 2) & 63) - 2 * jj + 1
            mask = (t >= 0) & (t < 4)
            v = jnp.broadcast_to(CC[p][None], (8, 16, 256))
            v = jnp.where(mask, v, 0.0).reshape(128, 256).astype(BF16)
            r = dot(v, V[par])
            z = row_before(r[:, 0:128]) + r[:, 128:256] + row_after(r[:, 256:384])
            sig = 1.0 / (1.0 + jnp.exp(-z))
            h = z * sig
            if keep is not None:
                h = h * keep
            H3[p, rows, 0:128] = row_before(h).astype(BF16)
            H3[p, rows, 128:256] = h.astype(BF16)
            H3[p, rows, 256:384] = row_after(h).astype(BF16)
            if p in (1, 2):
                dz = dh[p - 1, rows, :] * (sig * (1.0 + z * (1.0 - sig)))
                DZ3[p - 1, rows, 0:128] = row_after(dz).astype(BF16)
                DZ3[p - 1, rows, 128:256] = dz.astype(BF16)
                DZ3[p - 1, rows, 256:384] = row_before(dz).astype(BF16)

    for a in range(3):
        acc[a] = dot(GT[0], H3[a]) + dot(GT[1], H3[a + 1])

    spread = jnp.where((iota((16, ROWS), 1) & 15) == iota((16, ROWS), 0), 1.0, 0.0).astype(BF16)
    r_k = iota((256, ROWS), 0) & 63
    r_c = iota((256, ROWS), 1)
    jj = 2 * ((r_c & 255) // 16) + r_c // 256
    t = r_k - 2 * jj + 1
    near = (t >= 0) & (t < 4)
    for x in range(2):
        LT[x] = jnp.where(near, dot(CC[x + 1].T.astype(BF16), spread), 0.0).astype(BF16)
    parts = []
    for par in range(2):
        cols = slice(par * 256, par * 256 + 256)
        q = dot(LT[0, :, cols], DZ3[0, cols, :]) + dot(LT[1, :, cols], DZ3[1, cols, :])
        q = q.reshape(4, 8, 8, 384)
        parts.append([q[a].sum(0) for a in range(3)])
    d1[...] = jnp.zeros((64, 128), F32)
    for a in range(3):
        u, w = parts[0][a], parts[1][a]
        u = u + pltpu.roll(u, 4, 0)
        w = w + pltpu.roll(w, 4, 0)
        u = u + pltpu.roll(w, 2, 0)
        for b in range(3):
            v = u[:, b * 128 : (b + 1) * 128]
            v = pltpu.roll(v, 64, 1) + pltpu.roll(v, 7, 0)
            v = pltpu.roll(v, 1, 0)
            d1[9 * a + 3 * b : 9 * a + 3 * b + 3, :] = v[0:3]

    lane = iota((64, 128), 1)

    def term(o):
        a, b, c = o // 9, (o // 3) % 3, o % 3
        r = (2 - c) * 64
        cols = slice(b * 128, b * 128 + 128)
        v = jnp.where(lane < 64, acc[a, r : r + 64, cols], acc[a, r + 64 : r + 128, cols])
        return v + pltpu.roll(v, 64, 1)

    for q in range(14):
        other = term(2 * q + 1) if q < 13 else d1[...]
        v = jnp.where(lane < 64, term(2 * q), other)
        rsend[2 * q] = v[0:32].astype(BF16)
        rsend[2 * q + 1] = v[32:64].astype(BF16)

    def r1_send(m):
        return pltpu.make_async_remote_copy(
            src_ref=rsend.at[m], dst_ref=r1.at[me],
            send_sem=r1_ss.at[m], recv_sem=r1_rs.at[me],
            device_id=member(m), device_id_type=MESH,
        )

    def r1_recv(m):
        return pltpu.make_async_remote_copy(
            src_ref=rsend.at[0], dst_ref=r1.at[m],
            send_sem=r1_ss.at[0], recv_sem=r1_rs.at[m],
            device_id=member(m), device_id_type=MESH,
        )

    def r2_copy(k, slot):
        return pltpu.make_async_remote_copy(
            src_ref=r2.at[mez], dst_ref=r2.at[slot],
            send_sem=r2_ss.at[k], recv_sem=r2_rs.at[slot],
            device_id=zpeer(k), device_id_type=MESH,
        )

    def r3_copy(m, slot):
        return pltpu.make_async_remote_copy(
            src_ref=f3, dst_ref=r3.at[slot],
            send_sem=r3_ss.at[m], recv_sem=r3_rs.at[slot],
            device_id=member(m), device_id_type=MESH,
        )

    @pl.loop(1, GROUP)
    def _(k):
        m = lax.rem(me + k, GROUP)
        pl.when(m < CHUNKS)(lambda: r1_send(m).start())

    @pl.when(me < CHUNKS)
    def _():
        def add(k, total):
            m = lax.rem(me + k, GROUP)
            r1_recv(m).wait_recv()
            return total + r1[m].astype(F32)

        r2[mez] = lax.fori_loop(1, GROUP, add, rsend[me].astype(F32))

        @pl.loop(1, ZS)
        def _(k):
            r2_copy(lax.rem(mez + k, ZS), mez).start()

        @pl.loop(1, ZS)
        def _(k):
            m = lax.rem(mez + k, ZS)
            r2_copy(m, m).wait_recv()

        total = r2[0]
        for k in range(1, ZS):
            total = total + r2[k]
        f3[...] = total.astype(BF16)

        @pl.loop(1, GROUP)
        def _(k):
            r3_copy(lax.rem(me + k, GROUP), me).start()

        r3[me] = f3[...]

    @pl.loop(1, GROUP)
    def _(k):
        m = lax.rem(me + k, GROUP)
        pl.when(m < CHUNKS)(lambda: r3_copy(m, m).wait_recv())

    for q in range(14):
        v = jnp.concatenate([r3[2 * q], r3[2 * q + 1]], axis=0).astype(F32)
        if q < 13:
            dw2o[:, 128 * q : 128 * q + 128] = v
        else:
            dw2o[:, 128 * q : 128 * q + 64] = v[:, 0:64]
            dw1o[...] = pltpu.roll(v, 64, 1)[0:27, 0:64]

    stores[2].start()
    stores[3].start()

    for d in range(8):
        @pl.when(has(d))
        def _():
            ab_copy(d, True).wait_send()
            p_copy(0, d, True).wait_send()
            p_copy(1, d, True).wait_send()

    for side, ok in x_sides:
        @pl.when(ok)
        def _():
            fx_copy(side, True).wait_send()
            g_copy(side, True).wait_send()

    for side, ok in y_sides:
        pl.when(ok)(lambda side=side: fy_copy(side, True).wait_send())
    each_snap(0, GY, lambda d, s: sn_send(d, s).wait_send())

    @pl.loop(1, GROUP)
    def _(k):
        m = lax.rem(me + k, GROUP)
        pl.when(m < CHUNKS)(lambda: r1_send(m).wait_send())
        pl.when(me < CHUNKS)(lambda: r3_copy(m, me).wait_send())

    @pl.when(me < CHUNKS)
    def _():
        @pl.loop(1, ZS)
        def _(k):
            r2_copy(lax.rem(mez + k, ZS), mez).wait_send()

    for c in stores:
        c.wait()


def per_device(
    level_set, source, stiffness, snap_buffer, buffer_order, first_weight, second_weight, out_grad
):
    snap = snap_buffer.reshape(8, 4, 64)
    g = out_grad.reshape(2, 16, 4096)
    vm = pl.BlockSpec(memory_space=pltpu.VMEM)
    sm = pl.BlockSpec(memory_space=pltpu.SMEM)
    hbm = pl.BlockSpec(memory_space=pltpu.HBM)
    dma = pltpu.SemaphoreType.DMA
    shapes = (
        jax.ShapeDtypeStruct((8, 8, FZ), F32),
        jax.ShapeDtypeStruct((8, 8, FZ), F32),
        jax.ShapeDtypeStruct((27, 64), F32),
        jax.ShapeDtypeStruct((64, 1728), F32),
    )
    results = pl.pallas_call(
        kernel,
        out_shape=shapes,
        in_specs=[hbm, hbm, hbm, vm, sm, vm, hbm, hbm],
        out_specs=(hbm,) * 4,
        scratch_shapes=[
            pltpu.VMEM((8, 8, FZ), F32),
            pltpu.VMEM((8, 8, FZ), F32),
            pltpu.VMEM((27, 64), F32),
            pltpu.VMEM((64, 1728), F32),
            dma((4,)),
            pltpu.VMEM((8, 8, FZ), F32),
            pltpu.VMEM((8, 8, FZ), F32),
            pltpu.VMEM((8, 8, FZ), F32),
            pltpu.VMEM((64, 1728), BF16),
            pltpu.VMEM((2, 16, 4096), BF16),
            pltpu.VMEM((64, 1792), F32),
            dma((5,)),
            pltpu.VMEM((24, 24, FZ), F32),
            pltpu.VMEM((24, 24, FZ), F32),
            pltpu.VMEM((24, 24, FZ), F32),
            pltpu.VMEM((8, 16, FZ), BF16),
            pltpu.VMEM((8, 8, 16, FZ), BF16),
            pltpu.VMEM((2, 4, 16, FZ), BF16),
            pltpu.VMEM((2, 8, 4, 16, FZ), BF16),
            pltpu.VMEM((2, 8, FZ), F32),
            pltpu.VMEM((2, 8, FZ), F32),
            pltpu.VMEM((2, 8, FZ), F32),
            pltpu.VMEM((8, 8, 128), F32),
            pltpu.VMEM((3, 8, 8, 128), F32),
            pltpu.VMEM((2, 16, 4096), BF16),
            pltpu.VMEM((4, ROWS, 256), BF16),
            pltpu.VMEM((2, 256, ROWS), BF16),
            pltpu.VMEM((3, 256, 384), BF16),
            pltpu.VMEM((2, 256, 384), BF16),
            pltpu.VMEM((32, 128), F32),
            pltpu.VMEM((6, 16, 128), F32),
            pltpu.VMEM((4, 16, 256), F32),
            pltpu.VMEM((4, ROWS, 384), BF16),
            pltpu.VMEM((2, ROWS, 384), BF16),
            pltpu.VMEM((2, 256, ROWS), BF16),
            pltpu.VMEM((2, ROWS, 128), F32),
            pltpu.VMEM((3, 256, 384), F32),
            pltpu.VMEM((64, 128), F32),
            pltpu.VMEM((CHUNKS, 32, 128), BF16),
            pltpu.VMEM((GROUP, 32, 128), BF16),
            pltpu.VMEM((ZS, 32, 128), F32),
            pltpu.VMEM((32, 128), BF16),
            pltpu.VMEM((CHUNKS, 32, 128), BF16),
            dma((8,)), dma((8,)), dma((2, 8)), dma((2, 8)), dma((4,)), dma((4,)),
            dma((3, 8)), dma((3, 8)), dma((2,)), dma((2,)),
            dma((CHUNKS,)), dma((GROUP,)), dma((ZS,)), dma((ZS,)), dma((GROUP,)), dma((CHUNKS,)),
        ],
        compiler_params=pltpu.CompilerParams(
            collective_id=0, has_side_effects=True, vmem_limit_bytes=60 * 1024 * 1024
        ),
    )(source, stiffness, level_set, snap, buffer_order, first_weight, second_weight.T, g)
    return results[0], results[1], results[2], results[3].T


def solution(mesh):
    placed = (
        P("gx", "gy", None),
        P("gx", "gy", None),
        P("gx", "gy", None),
        P(None, "gx", "gy", None),
        P(),
        P(),
        P(),
        P("gy", "gx", None, None),
    )
    return jax.shard_map(
        per_device,
        mesh=mesh,
        in_specs=placed,
        out_specs=(P("gx", "gy", None), P("gx", "gy", None), P(), P()),
        check_vma=False,
    )
```

```python
import functools

import jax
import jax.numpy as jnp
from jax import lax
from jax.experimental import pallas as pl
from jax.experimental.pallas import tpu as pltpu
from jax.sharding import PartitionSpec as P

F32 = jnp.float32
BF16 = jnp.bfloat16
MESH = pl.DeviceIdType.MESH
GX, GY = 32, 8
FZ = 256
T = 8
ROWS = 512
RAD = 6
GROUP = 32
CHUNKS = 28
ZS = 8
DIRS = [(dx, dy) for dx in (-1, 0, 1) for dy in (-1, 0, 1) if (dx, dy) != (0, 0)]


def dot(a, b, dims=((1,), (0,)), precision=None):
    return lax.dot_general(
        a, b, (dims, ((), ())), preferred_element_type=F32, precision=precision
    )


def iota(shape, dim):
    return lax.broadcasted_iota(jnp.int32, shape, dim)


def tile_rows(dx, n):
    return {-1: (T - n, n), 0: (0, T), 1: (0, n)}[dx]


def row_before(v):
    y = iota(v.shape, 0) & 15
    return jnp.where(y == 0, 0.0, pltpu.roll(v, 1, 0))


def row_after(v):
    y = iota(v.shape, 0) & 15
    return jnp.where(y == 15, 0.0, pltpu.roll(v, v.shape[0] - 1, 0))


def z_before(v, axis):
    z = iota(v.shape, axis)
    return jnp.where(z == 0, 0.0, pltpu.roll(v, 1, axis))


def z_after(v, axis):
    z = iota(v.shape, axis)
    return jnp.where(z == FZ - 1, 0.0, pltpu.roll(v, FZ - 1, axis))


def kernel(
    src_h, stf_h, lev_h, snp, order, w1, w2_h, g_h,
    newl_h, prs_h, sum_h,
    newl, prs, out_s,
    src, stf, lev, w2, g, w2p, in_s,
    A, B, PP, absend, abrcv, psend, prcv, fysend, fxr, fyr,
    snsend, snrcv, grcv, W, GT, BT, V, w1s, S6, CC, H3, DZ3, LT, dh, acc, d1,
    rsend, r1, r2, f3, r3,
    ab_ss, ab_rs, p_ss, p_rs, f_ss, f_rs, sn_ss, sn_rs, g_ss, g_rs,
    r1_ss, r1_rs, r2_ss, r2_rs, r3_ss, r3_rs,
):
    i = lax.axis_index("gx")
    j = lax.axis_index("gy")
    has_l, has_r = i > 0, i < GX - 1
    has_x = {-1: has_l, 0: True, 1: has_r}
    has_y = {-1: j > 0, 0: True, 1: j < GY - 1}

    def has(d):
        dx, dy = DIRS[d]
        if dx == 0:
            return has_y[dy]
        if dy == 0:
            return has_x[dx]
        return jnp.logical_and(has_x[dx], has_y[dy])

    cy, czh, cc = i // 8, (i // 2) % 4, i % 2
    czl, cx = j // 4, j % 4
    me = cy * 8 + cc * 4 + cx
    mez = czh * 2 + czl

    def member(m):
        return ((m // 8) * 8 + czh * 2 + (m // 4) % 2, czl * 4 + m % 4)

    def zpeer(k):
        return (cy * 8 + (k // 2) * 2 + cc, (k % 2) * 4 + cx)

    loads = [
        pltpu.make_async_copy(a, b, in_s.at[k])
        for k, (a, b) in enumerate(
            ((src_h, src), (stf_h, stf), (lev_h, lev), (g_h, g), (w2_h, w2))
        )
    ]
    for c in loads:
        c.start()

    bar = pltpu.get_barrier_semaphore()

    def greet(dev):
        pl.semaphore_signal(bar, inc=1, device_id=dev, device_id_type=MESH)

    @pl.when(has_l)
    def _():
        @pl.loop(0, GY)
        def _(s):
            greet((i - 1, s))

    @pl.when(has_r)
    def _():
        @pl.loop(0, GY)
        def _(s):
            greet((i + 1, s))

    @pl.loop(1, GY)
    def _(k):
        greet((i, lax.rem(j + k, GY)))

    @pl.loop(1, GROUP)
    def _(k):
        greet(member(lax.rem(me + k, GROUP)))

    @pl.loop(1, ZS)
    def _(k):
        greet(zpeer(lax.rem(mez + k, ZS)))

    for c in loads[:4]:
        c.wait()
    a_own = 1.0 / (6.0 + stf[...])
    b_own = src[...] * a_own
    A[8:16, 8:16, :] = a_own
    B[8:16, 8:16, :] = b_own
    PP[8:16, 8:16, :] = b_own
    absend[...] = jnp.concatenate([a_own, b_own], axis=1).astype(BF16)
    fysend[0] = lev[:, 0, :]
    fysend[1] = lev[:, 7, :]
    zero_tile = jnp.zeros((T, T, FZ), F32)
    for d, (dx, dy) in enumerate(DIRS):
        xs, ys = pl.ds(8 + 8 * dx, 8), pl.ds(8 + 8 * dy, 8)

        @pl.when(jnp.logical_not(has(d)))
        def _():
            A[xs, ys, :] = zero_tile
            B[xs, ys, :] = zero_tile
            PP[xs, ys, :] = zero_tile

    @pl.when(jnp.logical_not(has_l))
    def _():
        fxr[0] = jnp.zeros((T, FZ), F32)
        snrcv[0] = jnp.zeros((GY, 8, 128), F32)
        grcv[0] = jnp.zeros((16, 4096), BF16)

    @pl.when(jnp.logical_not(has_r))
    def _():
        fxr[1] = jnp.zeros((T, FZ), F32)
        snrcv[2] = jnp.zeros((GY, 8, 128), F32)
        grcv[1] = jnp.zeros((16, 4096), BF16)

    @pl.when(j == 0)
    def _():
        fyr[0] = jnp.zeros((T, FZ), F32)

    @pl.when(j == GY - 1)
    def _():
        fyr[1] = jnp.zeros((T, FZ), F32)

    snsend[...] = jnp.zeros((8, 8, 128), F32)
    for s in range(1, 8):
        snsend[s, 0:4, 0:64] = snp[order[s]].astype(F32)

    n_bar = (GY - 1) + (GROUP - 1) + (ZS - 1)
    n_bar = n_bar + jnp.where(has_l, GY, 0) + jnp.where(has_r, GY, 0)
    pl.semaphore_wait(bar, n_bar)

    def ab_copy(d, to):
        dx, dy = DIRS[d]
        slot = 7 - d if to else d
        send_dx = dx if to else -dx
        lo, n = tile_rows(-send_dx, RAD if dy == 0 else RAD - 1)
        rows = pl.ds(lo, n)
        return pltpu.make_async_remote_copy(
            src_ref=absend.at[rows], dst_ref=abrcv.at[slot, rows],
            send_sem=ab_ss.at[d], recv_sem=ab_rs.at[slot],
            device_id=(i + dx, j + dy), device_id_type=MESH,
        )

    def p_copy(e, d, to):
        dx, dy = DIRS[d]
        slot = 7 - d if to else d
        lo, n = tile_rows(-dx if to else dx, 8 if dy == 0 else 6)
        rows = pl.ds(lo // 2, n // 2)
        return pltpu.make_async_remote_copy(
            src_ref=psend.at[e, rows], dst_ref=prcv.at[e, slot, rows],
            send_sem=p_ss.at[e, d], recv_sem=p_rs.at[e, slot],
            device_id=(i + dx, j + dy), device_id_type=MESH,
        )

    def fx_copy(side, to):
        slot = 1 - side if to else side
        return pltpu.make_async_remote_copy(
            src_ref=lev.at[0 if side == 0 else 7], dst_ref=fxr.at[slot],
            send_sem=f_ss.at[side], recv_sem=f_rs.at[slot],
            device_id=(i + (2 * side - 1), j), device_id_type=MESH,
        )

    def fy_copy(side, to):
        slot = 1 - side if to else side
        return pltpu.make_async_remote_copy(
            src_ref=fysend.at[side], dst_ref=fyr.at[slot],
            send_sem=f_ss.at[2 + side], recv_sem=f_rs.at[2 + slot],
            device_id=(i, j + (2 * side - 1)), device_id_type=MESH,
        )

    def g_copy(side, to):
        slot = 1 - side if to else side
        return pltpu.make_async_remote_copy(
            src_ref=g.at[side], dst_ref=grcv.at[slot],
            send_sem=g_ss.at[side], recv_sem=g_rs.at[slot],
            device_id=(i + (2 * side - 1), j), device_id_type=MESH,
        )

    def sn_send(d, s):
        return pltpu.make_async_remote_copy(
            src_ref=snsend.at[s], dst_ref=snrcv.at[1 - d, j],
            send_sem=sn_ss.at[d + 1, s], recv_sem=sn_rs.at[1 - d, j],
            device_id=(i + d, s), device_id_type=MESH,
        )

    def sn_recv(d, y):
        return pltpu.make_async_remote_copy(
            src_ref=snsend.at[0], dst_ref=snrcv.at[d + 1, y],
            send_sem=sn_ss.at[d + 1, 0], recv_sem=sn_rs.at[d + 1, y],
            device_id=(i, j), device_id_type=MESH,
        )

    x_sides = ((0, has_l), (1, has_r))
    y_sides = ((0, has_y[-1]), (1, has_y[1]))

    for d in range(8):
        pl.when(has(d))(lambda d=d: ab_copy(d, True).start())
    for side, ok in x_sides:
        pl.when(ok)(lambda side=side: fx_copy(side, True).start())
    for side, ok in y_sides:
        pl.when(ok)(lambda side=side: fy_copy(side, True).start())
    for side, ok in x_sides:
        pl.when(ok)(lambda side=side: g_copy(side, True).start())

    def each_snap(lo, hi, act):
        @pl.loop(lo, hi)
        def _(s):
            pl.when(has_l)(lambda: act(-1, s))
            pl.when(s != j)(lambda: act(0, s))
            pl.when(has_r)(lambda: act(1, s))

    each_snap(1, GY, lambda d, s: sn_send(d, s).start())

    loads[4].wait()
    w2p[:, 0:1728] = w2[...].astype(F32)
    even = w2p[...]
    odd = pltpu.roll(even, 64, 1)
    left = iota((64, 128), 1) < 64

    def pair(o):
        t = ((o + 1) // 2) * 128
        return (odd if o % 2 else even)[:, t : t + 128]

    for a in range(3):
        for b in range(3):
            o = 9 * a + 3 * b
            tiles = (
                jnp.where(left, pair(o + 2), 0.0),
                pair(o + 1),
                pair(o),
                jnp.where(left, 0.0, pair(o - 1)),
            )
            for k, v in enumerate(tiles):
                BT[a, 64 * k : 64 * k + 64, 128 * b : 128 * b + 128] = v.astype(BF16)

    w1s[...] = jnp.zeros((32, 128), F32)
    w1s[0:27, 0:64] = w1[...].astype(F32)
    w1d = w1s[...]
    w1d = jnp.concatenate([w1d, pltpu.roll(w1d, 64, 1)], axis=0).astype(BF16)
    for par in range(2):
        for b in range(3):
            k = iota((256, 64), 0)
            col = iota((256, 64), 1)
            zo = col // 32
            zi = ((k & 63) + 5 - 2 * par) & 3
            cz = zi - zo
            want = 9 * (k // 64) + 3 * b + cz
            hit = (col % 32 == want) & (cz >= 0) & (cz < 3) & (k < 192)
            V[par, :, b * 128 : (b + 1) * 128] = dot(
                jnp.where(hit, 1.0, 0.0).astype(BF16), w1d
            ).astype(BF16)

    lane128 = iota((16, 128), 1)

    def windows(plane, gv):
        gr = pltpu.roll(gv.astype(F32), 64, 1)
        for t in range(33):
            if t == 0:
                tile = jnp.where(lane128 >= 64, gr[:, 0:128], 0.0)
            elif t == 32:
                tile = jnp.where(lane128 < 64, gr[:, 0:128], 0.0)
            else:
                tile = gr[:, 128 * t : 128 * (t + 1)]
            tile = tile.astype(BF16)
            if t < 32:
                r = ((t % 2) * 16 + t // 2) * 16
                W[plane, r : r + 16, 0:128] = tile
            if t > 0:
                r = (((t - 1) % 2) * 16 + (t - 1) // 2) * 16
                W[plane, r : r + 16, 128:256] = tile

    for x in range(2):
        windows(x + 1, g[x])
        GT[x] = W[x + 1].T

    for d, (dx, dy) in enumerate(DIRS):
        lo, n = tile_rows(dx, RAD if dy == 0 else RAD - 1)
        xs, ys = pl.ds(8 + 8 * dx + lo, n), pl.ds(8 + 8 * dy, 8)

        @pl.when(has(d))
        def _():
            ab_copy(d, False).wait_recv()
            v = abrcv[d, lo : lo + n].astype(F32)
            A[xs, ys, :] = v[:, 0:8]
            B[xs, ys, :] = v[:, 8:16]
            PP[xs, ys, :] = v[:, 8:16]

    def around(v):
        rows = pltpu.roll(v, 1, 0) + pltpu.roll(v, 23, 0)
        return rows + z_before(v, 1) + z_after(v, 1)

    def sweeps(first, count):
        for rad in range(first, first - count, -1):
            lo, hi = 8 - rad, 16 + rad
            before, cur = PP[lo - 1], PP[lo]
            for x in range(lo, hi):
                after = PP[x + 1]
                PP[x] = B[x] + A[x] * (before + after + around(cur))
                before, cur = cur, after

    def exchange(e, filler):
        own = PP[8:16, 8:16, :]
        psend[e] = own.reshape(4, 16, FZ).astype(BF16)
        for d in range(8):
            pl.when(has(d))(lambda d=d: p_copy(e, d, True).start())
        filler()
        for d, (dx, dy) in enumerate(DIRS):
            lo, n = tile_rows(dx, 8 if dy == 0 else 6)
            xs, ys = pl.ds(8 + 8 * dx + lo, n), pl.ds(8 + 8 * dy, 8)

            @pl.when(has(d))
            def _():
                p_copy(e, d, False).wait_recv()
                v = prcv[e, d, lo // 2 : (lo + n) // 2].astype(F32)
                PP[xs, ys, :] = v.reshape(n, 8, FZ)

    def back(x):
        @pl.loop(0, 4)
        def _(q):
            rows = pl.ds(pl.multiple_of(q * 128, 128), 128)
            r = dot(W[x + 2, rows, :], BT[0])
            r = r + dot(W[x + 1, rows, :], BT[1])
            r = r + dot(W[x, rows, :], BT[2])
            dh[x, rows, :] = (
                row_after(r[:, 0:128]) + r[:, 128:256] + row_before(r[:, 256:384])
            )

    lane = iota((64, 128), 1)

    def term(o):
        a, b, c = o // 9, (o // 3) % 3, o % 3
        r = (2 - c) * 64
        cols = slice(b * 128, b * 128 + 128)
        v = jnp.where(lane < 64, acc[a, r : r + 64, cols], acc[a, r + 64 : r + 128, cols])
        return v + pltpu.roll(v, 64, 1)

    def r1_send(m):
        return pltpu.make_async_remote_copy(
            src_ref=rsend.at[m], dst_ref=r1.at[me],
            send_sem=r1_ss.at[m], recv_sem=r1_rs.at[me],
            device_id=member(m), device_id_type=MESH,
        )

    def r1_recv(m):
        return pltpu.make_async_remote_copy(
            src_ref=rsend.at[0], dst_ref=r1.at[m],
            send_sem=r1_ss.at[0], recv_sem=r1_rs.at[m],
            device_id=member(m), device_id_type=MESH,
        )

    def r2_copy(k, slot):
        return pltpu.make_async_remote_copy(
            src_ref=r2.at[mez], dst_ref=r2.at[slot],
            send_sem=r2_ss.at[k], recv_sem=r2_rs.at[slot],
            device_id=zpeer(k), device_id_type=MESH,
        )

    def r3_copy(m, slot):
        return pltpu.make_async_remote_copy(
            src_ref=f3, dst_ref=r3.at[slot],
            send_sem=r3_ss.at[m], recv_sem=r3_rs.at[slot],
            device_id=member(m), device_id_type=MESH,
        )

    def first_gradient():
        spread = jnp.where((iota((16, ROWS), 1) & 15) == iota((16, ROWS), 0), 1.0, 0.0).astype(BF16)
        r_k = iota((256, ROWS), 0) & 63
        r_c = iota((256, ROWS), 1)
        jj = 2 * ((r_c & 255) // 16) + r_c // 256
        t = r_k - 2 * jj + 1
        near = (t >= 0) & (t < 4)
        for x in range(2):
            LT[x] = jnp.where(near, dot(CC[x + 1].T.astype(BF16), spread), 0.0).astype(BF16)
        parts = []
        for par in range(2):
            cols = slice(par * 256, par * 256 + 256)
            q = dot(LT[0, :, cols], DZ3[0, cols, :]) + dot(LT[1, :, cols], DZ3[1, cols, :])
            q = q.reshape(4, 8, 8, 384)
            parts.append([q[a].sum(0) for a in range(3)])
        d1[...] = jnp.zeros((64, 128), F32)
        for a in range(3):
            u, w = parts[0][a], parts[1][a]
            u = u + pltpu.roll(u, 4, 0)
            w = w + pltpu.roll(w, 4, 0)
            u = u + pltpu.roll(w, 2, 0)
            for b in range(3):
                v = u[:, b * 128 : (b + 1) * 128]
                v = pltpu.roll(v, 64, 1) + pltpu.roll(v, 7, 0)
                v = pltpu.roll(v, 1, 0)
                d1[9 * a + 3 * b : 9 * a + 3 * b + 3, :] = v[0:3]

    def layers():
        snrcv[1, j] = snsend[j]
        @pl.when(has_l)
        def _():
            @pl.loop(0, GY)
            def _(y):
                sn_recv(-1, y).wait_recv()

        @pl.when(has_r)
        def _():
            @pl.loop(0, GY)
            def _(y):
                sn_recv(1, y).wait_recv()

        @pl.loop(1, GY)
        def _(k):
            sn_recv(0, lax.rem(j + k, GY)).wait_recv()

        for d in range(3):
            for y in range(8):
                t = snrcv[d, y]
                S6[2 * d, 2 * y : 2 * y + 2, :] = t[0:2]
                S6[2 * d + 1, 2 * y : 2 * y + 2, :] = t[2:4]
        for p in range(4):
            CC[p, :, 0:128] = S6[p] + pltpu.roll(S6[p + 1], 64, 1)
            CC[p, :, 128:256] = S6[p + 2]

        for p in range(4):
            keep = {0: jnp.where(has_l, 1.0, 0.0), 3: jnp.where(has_r, 1.0, 0.0)}.get(p)

            for q in range(4):
                rows = slice(q * 128, q * 128 + 128)
                par = q // 2
                jj = 2 * ((q % 2) * 8 + iota((8, 16, 256), 0)) + par
                t = (iota((8, 16, 256), 2) & 63) - 2 * jj + 1
                mask = (t >= 0) & (t < 4)
                v = jnp.broadcast_to(CC[p][None], (8, 16, 256))
                v = jnp.where(mask, v, 0.0).reshape(128, 256).astype(BF16)
                r = dot(v, V[par])
                z = row_before(r[:, 0:128]) + r[:, 128:256] + row_after(r[:, 256:384])
                sig = 1.0 / (1.0 + jnp.exp(-z))
                h = z * sig
                if keep is not None:
                    h = h * keep
                H3[p, rows, 0:128] = row_before(h).astype(BF16)
                H3[p, rows, 128:256] = h.astype(BF16)
                H3[p, rows, 256:384] = row_after(h).astype(BF16)
                if p in (1, 2):
                    dz = dh[p - 1, rows, :] * (sig * (1.0 + z * (1.0 - sig)))
                    DZ3[p - 1, rows, 0:128] = row_after(dz).astype(BF16)
                    DZ3[p - 1, rows, 128:256] = dz.astype(BF16)
                    DZ3[p - 1, rows, 256:384] = row_before(dz).astype(BF16)

        for a in range(3):
            acc[a] = dot(GT[0], H3[a]) + dot(GT[1], H3[a + 1])
            if a == 2:
                first_gradient()
            for q in range((0, 4, 9)[a], (4, 9, 14)[a]):
                other = term(2 * q + 1) if q < 13 else d1[...]
                v = jnp.where(lane < 64, term(2 * q), other)
                rsend[2 * q] = v[0:32].astype(BF16)
                rsend[2 * q + 1] = v[32:64].astype(BF16)
            c0, n = (0, 8, 18)[a], (8, 10, 10)[a]

            @pl.loop(0, n)
            def _(k):
                m = c0 + lax.rem(me + k, n)
                pl.when(m != me)(lambda: r1_send(m).start())

    def filler_one():
        for side, ok in x_sides:
            pl.when(ok)(lambda side=side: g_copy(side, False).wait_recv())
        windows(0, grcv[0])
        windows(3, grcv[1])
        back(0)
        back(1)

    def filler_two():
        pl.when(j > 0)(layers)

    sweeps(RAD - 1, RAD)
    exchange(0, filler_one)
    sweeps(6, 7)
    exchange(1, filler_two)
    sweeps(6, 6)

    for side, ok in x_sides:
        pl.when(ok)(lambda side=side: fx_copy(side, False).wait_recv())
    for side, ok in y_sides:
        pl.when(ok)(lambda side=side: fy_copy(side, False).wait_recv())

    pool = jnp.where(iota((FZ, 128), 0) // 4 == iota((FZ, 128), 1), 1.0 / 64.0, 0.0).astype(BF16)
    row8 = iota((8, FZ), 0)
    sums = []
    total = None
    for x in range(8):
        pc = PP[x + 8]
        px = 0.5 * (PP[x + 9, 8:16] - PP[x + 7, 8:16])
        py = 0.5 * (pltpu.roll(pc, 23, 0) - pltpu.roll(pc, 1, 0))[8:16]
        pm = pc[8:16]
        pz = 0.5 * (z_after(pm, 1) - z_before(pm, 1))
        fm = lev[x]
        f_lo = fxr[0] if x == 0 else lev[x - 1]
        f_hi = fxr[1] if x == 7 else lev[x + 1]
        fx = 0.5 * (f_hi - f_lo)
        y_lo = jnp.where(row8 == 0, fyr[0, x : x + 1, :], pltpu.roll(fm, 1, 0))
        y_hi = jnp.where(row8 == 7, fyr[1, x : x + 1, :], pltpu.roll(fm, 7, 0))
        fy = 0.5 * (y_hi - y_lo)
        fz = 0.5 * (z_after(fm, 1) - z_before(fm, 1))
        new = fm + 2.0 * (px * fx + py * fy + pz * fz)
        newl[x] = new
        prs[x] = pm
        total = new if x % 4 == 0 else total + new
        if x % 4 == 3:
            t = total + pltpu.roll(total, 7, 0)
            sums.append(t + pltpu.roll(t, 6, 0))
    rest, mean = jnp.concatenate(sums, axis=0), 0.0
    for _ in range(3):
        part = rest.astype(BF16)
        rest = rest - part.astype(F32)
        mean = mean + dot(part, pool)
    for r in range(4):
        snsend[0, r : r + 1, :] = mean[4 * r : 4 * r + 1, :]
    snsend[0, 4:8, :] = jnp.zeros((4, 128), F32)

    each_snap(0, 1, lambda d, s: sn_send(d, s).start())
    stores = [
        pltpu.make_async_copy(a, b, out_s.at[k])
        for k, (a, b) in enumerate(
            ((newl, newl_h), (prs, prs_h), (r3, sum_h))
        )
    ]
    stores[0].start()
    stores[1].start()
    pl.when(j == 0)(layers)

    @pl.when(me < CHUNKS)
    def _():
        def add(k, total):
            m = lax.rem(me + k, GROUP)
            r1_recv(m).wait_recv()
            return total + r1[m].astype(F32)

        r2[mez] = lax.fori_loop(1, GROUP, add, rsend[me].astype(F32))

        @pl.loop(1, ZS)
        def _(k):
            r2_copy(lax.rem(mez + k, ZS), mez).start()

        @pl.loop(1, ZS)
        def _(k):
            m = lax.rem(mez + k, ZS)
            r2_copy(m, m).wait_recv()

        total = r2[0]
        for k in range(1, ZS):
            total = total + r2[k]
        f3[...] = total.astype(BF16)

        @pl.loop(1, GROUP)
        def _(k):
            r3_copy(lax.rem(me + k, GROUP), me).start()

        r3[me] = f3[...]

    @pl.loop(1, GROUP)
    def _(k):
        m = lax.rem(me + k, GROUP)
        pl.when(m < CHUNKS)(lambda: r3_copy(m, m).wait_recv())

    stores[2].start()

    for d in range(8):
        @pl.when(has(d))
        def _():
            ab_copy(d, True).wait_send()
            p_copy(0, d, True).wait_send()
            p_copy(1, d, True).wait_send()

    for side, ok in x_sides:
        @pl.when(ok)
        def _():
            fx_copy(side, True).wait_send()
            g_copy(side, True).wait_send()

    for side, ok in y_sides:
        pl.when(ok)(lambda side=side: fy_copy(side, True).wait_send())
    each_snap(0, GY, lambda d, s: sn_send(d, s).wait_send())

    @pl.loop(1, GROUP)
    def _(k):
        m = lax.rem(me + k, GROUP)
        pl.when(m < CHUNKS)(lambda: r1_send(m).wait_send())
        pl.when(me < CHUNKS)(lambda: r3_copy(m, me).wait_send())

    @pl.when(me < CHUNKS)
    def _():
        @pl.loop(1, ZS)
        def _(k):
            r2_copy(lax.rem(mez + k, ZS), mez).wait_send()

    for c in stores:
        c.wait()


def leave(
    newl_h, prs_h, sum_h, newl_o, prs_o, dw1_o, dw2_o,
    newl, prs, total, dw1, dw2, in_s, out_s,
):
    ins = [
        pltpu.make_async_copy(a, b, in_s.at[k])
        for k, (a, b) in enumerate(((sum_h, total), (newl_h, newl), (prs_h, prs)))
    ]
    outs = [
        pltpu.make_async_copy(a, b, out_s.at[k])
        for k, (a, b) in enumerate(
            ((newl, newl_o), (prs, prs_o), (dw1, dw1_o), (dw2, dw2_o))
        )
    ]
    for c in ins:
        c.start()
    ins[0].wait()
    for q in range(14):
        v = jnp.concatenate([total[2 * q], total[2 * q + 1]], axis=0).astype(F32)
        if q < 13:
            dw2[:, 128 * q : 128 * q + 128] = v
        else:
            dw2[:, 128 * q : 128 * q + 64] = v[:, 0:64]
            dw1[...] = pltpu.roll(v, 64, 1)[0:27, 0:64]
    outs[3].start()
    outs[2].start()
    ins[1].wait()
    outs[0].start()
    ins[2].wait()
    outs[1].start()
    for c in outs:
        c.wait()


def per_device(
    level_set, source, stiffness, snap_buffer, buffer_order, first_weight, second_weight, out_grad
):
    snap = snap_buffer.reshape(8, 4, 64)
    g = out_grad.reshape(2, 16, 4096)
    vm = pl.BlockSpec(memory_space=pltpu.VMEM)
    sm = pl.BlockSpec(memory_space=pltpu.SMEM)
    hbm = pl.BlockSpec(memory_space=pltpu.HBM)
    dma = pltpu.SemaphoreType.DMA
    shapes = (
        jax.ShapeDtypeStruct((8, 8, FZ), F32),
        jax.ShapeDtypeStruct((8, 8, FZ), F32),
        jax.ShapeDtypeStruct((27, 64), F32),
        jax.ShapeDtypeStruct((64, 1728), F32),
    )
    sums = jax.ShapeDtypeStruct((CHUNKS, 32, 128), BF16)
    results = pl.pallas_call(
        kernel,
        out_shape=shapes[:2] + (sums,),
        in_specs=[hbm, hbm, hbm, vm, sm, vm, hbm, hbm],
        out_specs=(hbm,) * 3,
        scratch_shapes=[
            pltpu.VMEM((8, 8, FZ), F32),
            pltpu.VMEM((8, 8, FZ), F32),
            dma((3,)),
            pltpu.VMEM((8, 8, FZ), F32),
            pltpu.VMEM((8, 8, FZ), F32),
            pltpu.VMEM((8, 8, FZ), F32),
            pltpu.VMEM((64, 1728), BF16),
            pltpu.VMEM((2, 16, 4096), BF16),
            pltpu.VMEM((64, 1792), F32),
            dma((5,)),
            pltpu.VMEM((24, 24, FZ), F32),
            pltpu.VMEM((24, 24, FZ), F32),
            pltpu.VMEM((24, 24, FZ), F32),
            pltpu.VMEM((8, 16, FZ), BF16),
            pltpu.VMEM((8, 8, 16, FZ), BF16),
            pltpu.VMEM((2, 4, 16, FZ), BF16),
            pltpu.VMEM((2, 8, 4, 16, FZ), BF16),
            pltpu.VMEM((2, 8, FZ), F32),
            pltpu.VMEM((2, 8, FZ), F32),
            pltpu.VMEM((2, 8, FZ), F32),
            pltpu.VMEM((8, 8, 128), F32),
            pltpu.VMEM((3, 8, 8, 128), F32),
            pltpu.VMEM((2, 16, 4096), BF16),
            pltpu.VMEM((4, ROWS, 256), BF16),
            pltpu.VMEM((2, 256, ROWS), BF16),
            pltpu.VMEM((3, 256, 384), BF16),
            pltpu.VMEM((2, 256, 384), BF16),
            pltpu.VMEM((32, 128), F32),
            pltpu.VMEM((6, 16, 128), F32),
            pltpu.VMEM((4, 16, 256), F32),
            pltpu.VMEM((4, ROWS, 384), BF16),
            pltpu.VMEM((2, ROWS, 384), BF16),
            pltpu.VMEM((2, 256, ROWS), BF16),
            pltpu.VMEM((2, ROWS, 128), F32),
            pltpu.VMEM((3, 256, 384), F32),
            pltpu.VMEM((64, 128), F32),
            pltpu.VMEM((CHUNKS, 32, 128), BF16),
            pltpu.VMEM((GROUP, 32, 128), BF16),
            pltpu.VMEM((ZS, 32, 128), F32),
            pltpu.VMEM((32, 128), BF16),
            pltpu.VMEM((CHUNKS, 32, 128), BF16),
            dma((8,)), dma((8,)), dma((2, 8)), dma((2, 8)), dma((4,)), dma((4,)),
            dma((3, 8)), dma((3, 8)), dma((2,)), dma((2,)),
            dma((CHUNKS,)), dma((GROUP,)), dma((ZS,)), dma((ZS,)), dma((GROUP,)), dma((CHUNKS,)),
        ],
        compiler_params=pltpu.CompilerParams(
            collective_id=0, has_side_effects=True, vmem_limit_bytes=60 * 1024 * 1024
        ),
    )(source, stiffness, level_set, snap, buffer_order, first_weight, second_weight.T, g)
    results = pl.pallas_call(
        leave,
        out_shape=shapes,
        in_specs=[hbm] * 3,
        out_specs=(hbm,) * 4,
        scratch_shapes=[
            pltpu.VMEM(shapes[0].shape, F32),
            pltpu.VMEM(shapes[1].shape, F32),
            pltpu.VMEM(sums.shape, BF16),
            pltpu.VMEM(shapes[2].shape, F32),
            pltpu.VMEM(shapes[3].shape, F32),
            dma((3,)),
            dma((4,)),
        ],
        compiler_params=pltpu.CompilerParams(vmem_limit_bytes=60 * 1024 * 1024),
    )(*results)
    return results[0], results[1], results[2], results[3].T


def solution(mesh):
    placed = (
        P("gx", "gy", None),
        P("gx", "gy", None),
        P("gx", "gy", None),
        P(None, "gx", "gy", None),
        P(),
        P(),
        P(),
        P("gy", "gx", None, None),
    )
    return jax.shard_map(
        per_device,
        mesh=mesh,
        in_specs=placed,
        out_specs=(P("gx", "gy", None), P("gx", "gy", None), P(), P()),
        check_vma=False,
    )
```

```python
import functools

import jax
import jax.numpy as jnp
from jax import lax
from jax.experimental import pallas as pl
from jax.experimental.pallas import tpu as pltpu
from jax.sharding import PartitionSpec as P

F32 = jnp.float32
BF16 = jnp.bfloat16
MESH = pl.DeviceIdType.MESH
GX, GY = 32, 8
FZ = 256
T = 8
ROWS = 512
RAD = 6
GROUP = 32
CHUNKS = 28
ZS = 8
DIRS = [(dx, dy) for dx in (-1, 0, 1) for dy in (-1, 0, 1) if (dx, dy) != (0, 0)]


def dot(a, b, dims=((1,), (0,)), precision=None):
    return lax.dot_general(
        a, b, (dims, ((), ())), preferred_element_type=F32, precision=precision
    )


def iota(shape, dim):
    return lax.broadcasted_iota(jnp.int32, shape, dim)


def tile_rows(dx, n):
    return {-1: (T - n, n), 0: (0, T), 1: (0, n)}[dx]


def row_before(v):
    y = iota(v.shape, 0) & 15
    return jnp.where(y == 0, 0.0, pltpu.roll(v, 1, 0))


def row_after(v):
    y = iota(v.shape, 0) & 15
    return jnp.where(y == 15, 0.0, pltpu.roll(v, v.shape[0] - 1, 0))


def z_before(v, axis):
    z = iota(v.shape, axis)
    return jnp.where(z == 0, 0.0, pltpu.roll(v, 1, axis))


def z_after(v, axis):
    z = iota(v.shape, axis)
    return jnp.where(z == FZ - 1, 0.0, pltpu.roll(v, FZ - 1, axis))


def kernel(
    src_h, stf_h, lev_h, snp, order, w1, w2_h, g_h,
    newl_h, prs_h, sum_h,
    newl, prs, out_s,
    src, stf, lev, w2, g, w2p, in_s,
    A, B, PP, absend, abrcv, psend, prcv, fysend, fxr, fyr,
    snsend, snrcv, grcv, W, GT, BT, V, w1s, S6, CC, H3, DZ3, LT, dh, acc, d1,
    rsend, r1, r2, f3, r3,
    ab_ss, ab_rs, p_ss, p_rs, f_ss, f_rs, sn_ss, sn_rs, g_ss, g_rs,
    r1_ss, r1_rs, r2_ss, r2_rs, r3_ss, r3_rs,
):
    i = lax.axis_index("gx")
    j = lax.axis_index("gy")
    has_l, has_r = i > 0, i < GX - 1
    has_x = {-1: has_l, 0: True, 1: has_r}
    has_y = {-1: j > 0, 0: True, 1: j < GY - 1}

    def has(d):
        dx, dy = DIRS[d]
        if dx == 0:
            return has_y[dy]
        if dy == 0:
            return has_x[dx]
        return jnp.logical_and(has_x[dx], has_y[dy])

    cy, czh, cc = i // 8, (i // 2) % 4, i % 2
    czl, cx = j // 4, j % 4
    me = cy * 8 + cc * 4 + cx
    mez = czh * 2 + czl
    mine = lax.rem(3 * me, GROUP)

    def member(m):
        return ((m // 8) * 8 + czh * 2 + (m // 4) % 2, czl * 4 + m % 4)

    def zpeer(k):
        return (cy * 8 + (k // 2) * 2 + cc, (k % 2) * 4 + cx)

    loads = [
        pltpu.make_async_copy(a, b, in_s.at[k])
        for k, (a, b) in enumerate(
            ((src_h, src), (stf_h, stf), (lev_h, lev), (g_h, g), (w2_h, w2))
        )
    ]
    for c in loads:
        c.start()

    bar = pltpu.get_barrier_semaphore()

    def greet(dev):
        pl.semaphore_signal(bar, inc=1, device_id=dev, device_id_type=MESH)

    @pl.loop(1, ZS)
    def _(k):
        greet(zpeer(lax.rem(mez + k, ZS)))

    @pl.loop(1, GROUP)
    def _(k):
        greet(member(lax.rem(me + k, GROUP)))

    @pl.when(has_l)
    def _():
        @pl.loop(0, GY)
        def _(s):
            greet((i - 1, s))

    @pl.when(has_r)
    def _():
        @pl.loop(0, GY)
        def _(s):
            greet((i + 1, s))

    @pl.loop(1, GY)
    def _(k):
        greet((i, lax.rem(j + k, GY)))


    for c in loads[:4]:
        c.wait()
    a_own = 1.0 / (6.0 + stf[...])
    b_own = src[...] * a_own
    A[8:16, 8:16, :] = a_own
    B[8:16, 8:16, :] = b_own
    PP[8:16, 8:16, :] = b_own
    absend[...] = jnp.concatenate([a_own, b_own], axis=1).astype(BF16)
    fysend[0] = lev[:, 0, :]
    fysend[1] = lev[:, 7, :]
    zero_tile = jnp.zeros((T, T, FZ), F32)
    for d, (dx, dy) in enumerate(DIRS):
        xs, ys = pl.ds(8 + 8 * dx, 8), pl.ds(8 + 8 * dy, 8)

        @pl.when(jnp.logical_not(has(d)))
        def _():
            A[xs, ys, :] = zero_tile
            B[xs, ys, :] = zero_tile
            PP[xs, ys, :] = zero_tile

    @pl.when(jnp.logical_not(has_l))
    def _():
        fxr[0] = jnp.zeros((T, FZ), F32)
        snrcv[0] = jnp.zeros((GY, 8, 128), F32)
        grcv[0] = jnp.zeros((16, 4096), BF16)

    @pl.when(jnp.logical_not(has_r))
    def _():
        fxr[1] = jnp.zeros((T, FZ), F32)
        snrcv[2] = jnp.zeros((GY, 8, 128), F32)
        grcv[1] = jnp.zeros((16, 4096), BF16)

    @pl.when(j == 0)
    def _():
        fyr[0] = jnp.zeros((T, FZ), F32)

    @pl.when(j == GY - 1)
    def _():
        fyr[1] = jnp.zeros((T, FZ), F32)

    snsend[...] = jnp.zeros((8, 8, 128), F32)
    for s in range(1, 8):
        snsend[s, 0:4, 0:64] = snp[order[s]].astype(F32)

    n_bar = (GY - 1) + (GROUP - 1) + (ZS - 1)
    n_bar = n_bar + jnp.where(has_l, GY, 0) + jnp.where(has_r, GY, 0)
    pl.semaphore_wait(bar, n_bar)

    def ab_copy(d, to):
        dx, dy = DIRS[d]
        slot = 7 - d if to else d
        send_dx = dx if to else -dx
        lo, n = tile_rows(-send_dx, RAD if dy == 0 else RAD - 1)
        rows = pl.ds(lo, n)
        return pltpu.make_async_remote_copy(
            src_ref=absend.at[rows], dst_ref=abrcv.at[slot, rows],
            send_sem=ab_ss.at[d], recv_sem=ab_rs.at[slot],
            device_id=(i + dx, j + dy), device_id_type=MESH,
        )

    def p_copy(e, d, to):
        dx, dy = DIRS[d]
        slot = 7 - d if to else d
        lo, n = tile_rows(-dx if to else dx, 8 if dy == 0 else 6)
        rows = pl.ds(lo // 2, n // 2)
        return pltpu.make_async_remote_copy(
            src_ref=psend.at[e, rows], dst_ref=prcv.at[e, slot, rows],
            send_sem=p_ss.at[e, d], recv_sem=p_rs.at[e, slot],
            device_id=(i + dx, j + dy), device_id_type=MESH,
        )

    def fx_copy(side, to):
        slot = 1 - side if to else side
        return pltpu.make_async_remote_copy(
            src_ref=lev.at[0 if side == 0 else 7], dst_ref=fxr.at[slot],
            send_sem=f_ss.at[side], recv_sem=f_rs.at[slot],
            device_id=(i + (2 * side - 1), j), device_id_type=MESH,
        )

    def fy_copy(side, to):
        slot = 1 - side if to else side
        return pltpu.make_async_remote_copy(
            src_ref=fysend.at[side], dst_ref=fyr.at[slot],
            send_sem=f_ss.at[2 + side], recv_sem=f_rs.at[2 + slot],
            device_id=(i, j + (2 * side - 1)), device_id_type=MESH,
        )

    def g_copy(side, to):
        slot = 1 - side if to else side
        return pltpu.make_async_remote_copy(
            src_ref=g.at[side], dst_ref=grcv.at[slot],
            send_sem=g_ss.at[side], recv_sem=g_rs.at[slot],
            device_id=(i + (2 * side - 1), j), device_id_type=MESH,
        )

    def sn_send(d, s):
        return pltpu.make_async_remote_copy(
            src_ref=snsend.at[s], dst_ref=snrcv.at[1 - d, j],
            send_sem=sn_ss.at[d + 1, s], recv_sem=sn_rs.at[1 - d, j],
            device_id=(i + d, s), device_id_type=MESH,
        )

    def sn_recv(d, y):
        return pltpu.make_async_remote_copy(
            src_ref=snsend.at[0], dst_ref=snrcv.at[d + 1, y],
            send_sem=sn_ss.at[d + 1, 0], recv_sem=sn_rs.at[d + 1, y],
            device_id=(i, j), device_id_type=MESH,
        )

    x_sides = ((0, has_l), (1, has_r))
    y_sides = ((0, has_y[-1]), (1, has_y[1]))

    for d in range(8):
        pl.when(has(d))(lambda d=d: ab_copy(d, True).start())
    for side, ok in x_sides:
        pl.when(ok)(lambda side=side: fx_copy(side, True).start())
    for side, ok in y_sides:
        pl.when(ok)(lambda side=side: fy_copy(side, True).start())
    def each_snap(lo, hi, act):
        @pl.loop(lo, hi)
        def _(s):
            pl.when(has_l)(lambda: act(-1, s))
            pl.when(s != j)(lambda: act(0, s))
            pl.when(has_r)(lambda: act(1, s))


    loads[4].wait()
    w2p[:, 0:1728] = w2[...].astype(F32)
    even = w2p[...]
    odd = pltpu.roll(even, 64, 1)
    left = iota((64, 128), 1) < 64

    def pair(o):
        t = ((o + 1) // 2) * 128
        return (odd if o % 2 else even)[:, t : t + 128]

    for a in range(3):
        for b in range(3):
            o = 9 * a + 3 * b
            tiles = (
                jnp.where(left, pair(o + 2), 0.0),
                pair(o + 1),
                pair(o),
                jnp.where(left, 0.0, pair(o - 1)),
            )
            for k, v in enumerate(tiles):
                BT[a, 64 * k : 64 * k + 64, 128 * b : 128 * b + 128] = v.astype(BF16)

    w1s[...] = jnp.zeros((32, 128), F32)
    w1s[0:27, 0:64] = w1[...].astype(F32)
    w1d = w1s[...]
    w1d = jnp.concatenate([w1d, pltpu.roll(w1d, 64, 1)], axis=0).astype(BF16)
    for par in range(2):
        for b in range(3):
            k = iota((256, 64), 0)
            col = iota((256, 64), 1)
            zo = col // 32
            zi = ((k & 63) + 5 - 2 * par) & 3
            cz = zi - zo
            want = 9 * (k // 64) + 3 * b + cz
            hit = (col % 32 == want) & (cz >= 0) & (cz < 3) & (k < 192)
            V[par, :, b * 128 : (b + 1) * 128] = dot(
                jnp.where(hit, 1.0, 0.0).astype(BF16), w1d
            ).astype(BF16)

    lane128 = iota((16, 128), 1)

    def windows(plane, gv):
        gr = pltpu.roll(gv.astype(F32), 64, 1)
        for t in range(33):
            if t == 0:
                tile = jnp.where(lane128 >= 64, gr[:, 0:128], 0.0)
            elif t == 32:
                tile = jnp.where(lane128 < 64, gr[:, 0:128], 0.0)
            else:
                tile = gr[:, 128 * t : 128 * (t + 1)]
            tile = tile.astype(BF16)
            if t < 32:
                r = ((t % 2) * 16 + t // 2) * 16
                W[plane, r : r + 16, 0:128] = tile
            if t > 0:
                r = (((t - 1) % 2) * 16 + (t - 1) // 2) * 16
                W[plane, r : r + 16, 128:256] = tile

    for d, (dx, dy) in enumerate(DIRS):
        lo, n = tile_rows(dx, RAD if dy == 0 else RAD - 1)
        xs, ys = pl.ds(8 + 8 * dx + lo, n), pl.ds(8 + 8 * dy, 8)

        @pl.when(has(d))
        def _():
            ab_copy(d, False).wait_recv()
            v = abrcv[d, lo : lo + n].astype(F32)
            A[xs, ys, :] = v[:, 0:8]
            B[xs, ys, :] = v[:, 8:16]
            PP[xs, ys, :] = v[:, 8:16]

    def around(v):
        rows = pltpu.roll(v, 1, 0) + pltpu.roll(v, 23, 0)
        return rows + z_before(v, 1) + z_after(v, 1)

    def sweeps(first, count):
        for rad in range(first, first - count, -1):
            lo, hi = 8 - rad, 16 + rad
            before, cur = PP[lo - 1], PP[lo]
            for x in range(lo, hi):
                after = PP[x + 1]
                PP[x] = B[x] + A[x] * (before + after + around(cur))
                before, cur = cur, after

    def exchange(e, filler):
        own = PP[8:16, 8:16, :]
        psend[e] = own.reshape(4, 16, FZ).astype(BF16)
        for d in range(8):
            pl.when(has(d))(lambda d=d: p_copy(e, d, True).start())
        filler()
        for d, (dx, dy) in enumerate(DIRS):
            lo, n = tile_rows(dx, 8 if dy == 0 else 6)
            xs, ys = pl.ds(8 + 8 * dx + lo, n), pl.ds(8 + 8 * dy, 8)

            @pl.when(has(d))
            def _():
                p_copy(e, d, False).wait_recv()
                v = prcv[e, d, lo // 2 : (lo + n) // 2].astype(F32)
                PP[xs, ys, :] = v.reshape(n, 8, FZ)

    def back(x):
        @pl.loop(0, 4)
        def _(q):
            rows = pl.ds(pl.multiple_of(q * 128, 128), 128)
            r = dot(W[x + 2, rows, :], BT[0])
            r = r + dot(W[x + 1, rows, :], BT[1])
            r = r + dot(W[x, rows, :], BT[2])
            dh[x, rows, :] = (
                row_after(r[:, 0:128]) + r[:, 128:256] + row_before(r[:, 256:384])
            )

    lane = iota((64, 128), 1)

    def term(o):
        a, b, c = o // 9, (o // 3) % 3, o % 3
        r = (2 - c) * 64
        cols = slice(b * 128, b * 128 + 128)
        v = jnp.where(lane < 64, acc[a, r : r + 64, cols], acc[a, r + 64 : r + 128, cols])
        return v + pltpu.roll(v, 64, 1)

    def r1_send(m):
        return pltpu.make_async_remote_copy(
            src_ref=rsend.at[m], dst_ref=r1.at[me],
            send_sem=r1_ss.at[m], recv_sem=r1_rs.at[me],
            device_id=member(lax.rem(11 * m, GROUP)), device_id_type=MESH,
        )

    def r1_recv(m):
        return pltpu.make_async_remote_copy(
            src_ref=rsend.at[0], dst_ref=r1.at[m],
            send_sem=r1_ss.at[0], recv_sem=r1_rs.at[m],
            device_id=member(m), device_id_type=MESH,
        )

    def r2_copy(k, slot):
        return pltpu.make_async_remote_copy(
            src_ref=r2.at[mez], dst_ref=r2.at[slot],
            send_sem=r2_ss.at[k], recv_sem=r2_rs.at[slot],
            device_id=zpeer(k), device_id_type=MESH,
        )

    def r3_copy(m, slot):
        return pltpu.make_async_remote_copy(
            src_ref=f3, dst_ref=r3.at[slot],
            send_sem=r3_ss.at[m], recv_sem=r3_rs.at[slot],
            device_id=member(m), device_id_type=MESH,
        )

    def first_gradient():
        spread = jnp.where((iota((16, ROWS), 1) & 15) == iota((16, ROWS), 0), 1.0, 0.0).astype(BF16)
        r_k = iota((256, ROWS), 0) & 63
        r_c = iota((256, ROWS), 1)
        jj = 2 * ((r_c & 255) // 16) + r_c // 256
        t = r_k - 2 * jj + 1
        near = (t >= 0) & (t < 4)
        for x in range(2):
            LT[x] = jnp.where(near, dot(CC[x + 1].T.astype(BF16), spread), 0.0).astype(BF16)
        parts = []
        for par in range(2):
            cols = slice(par * 256, par * 256 + 256)
            q = dot(LT[0, :, cols], DZ3[0, cols, :]) + dot(LT[1, :, cols], DZ3[1, cols, :])
            q = q.reshape(4, 8, 8, 384)
            parts.append([q[a].sum(0) for a in range(3)])
        d1[...] = jnp.zeros((64, 128), F32)
        for a in range(3):
            u, w = parts[0][a], parts[1][a]
            u = u + pltpu.roll(u, 4, 0)
            w = w + pltpu.roll(w, 4, 0)
            u = u + pltpu.roll(w, 2, 0)
            for b in range(3):
                v = u[:, b * 128 : (b + 1) * 128]
                v = pltpu.roll(v, 64, 1) + pltpu.roll(v, 7, 0)
                v = pltpu.roll(v, 1, 0)
                d1[9 * a + 3 * b : 9 * a + 3 * b + 3, :] = v[0:3]

    def layers():
        snrcv[1, j] = snsend[j]
        @pl.when(has_l)
        def _():
            @pl.loop(0, GY)
            def _(y):
                sn_recv(-1, y).wait_recv()

        @pl.when(has_r)
        def _():
            @pl.loop(0, GY)
            def _(y):
                sn_recv(1, y).wait_recv()

        @pl.loop(1, GY)
        def _(k):
            sn_recv(0, lax.rem(j + k, GY)).wait_recv()

        for d in range(3):
            for y in range(8):
                t = snrcv[d, y]
                S6[2 * d, 2 * y : 2 * y + 2, :] = t[0:2]
                S6[2 * d + 1, 2 * y : 2 * y + 2, :] = t[2:4]
        for p in range(4):
            CC[p, :, 0:128] = S6[p] + pltpu.roll(S6[p + 1], 64, 1)
            CC[p, :, 128:256] = S6[p + 2]

        for p in range(4):
            keep = {0: jnp.where(has_l, 1.0, 0.0), 3: jnp.where(has_r, 1.0, 0.0)}.get(p)

            for q in range(4):
                rows = slice(q * 128, q * 128 + 128)
                par = q // 2
                jj = 2 * ((q % 2) * 8 + iota((8, 16, 256), 0)) + par
                t = (iota((8, 16, 256), 2) & 63) - 2 * jj + 1
                mask = (t >= 0) & (t < 4)
                v = jnp.broadcast_to(CC[p][None], (8, 16, 256))
                v = jnp.where(mask, v, 0.0).reshape(128, 256).astype(BF16)
                r = dot(v, V[par])
                z = row_before(r[:, 0:128]) + r[:, 128:256] + row_after(r[:, 256:384])
                sig = 1.0 / (1.0 + jnp.exp(-z))
                h = z * sig
                if keep is not None:
                    h = h * keep
                H3[p, rows, 0:128] = row_before(h).astype(BF16)
                H3[p, rows, 128:256] = h.astype(BF16)
                H3[p, rows, 256:384] = row_after(h).astype(BF16)
                if p in (1, 2):
                    dz = dh[p - 1, rows, :] * (sig * (1.0 + z * (1.0 - sig)))
                    DZ3[p - 1, rows, 0:128] = row_after(dz).astype(BF16)
                    DZ3[p - 1, rows, 128:256] = dz.astype(BF16)
                    DZ3[p - 1, rows, 256:384] = row_before(dz).astype(BF16)

        for a in range(3):
            acc[a] = dot(GT[0], H3[a]) + dot(GT[1], H3[a + 1])
            if a == 2:
                first_gradient()
            for q in range((0, 4, 9)[a], (4, 9, 14)[a]):
                other = term(2 * q + 1) if q < 13 else d1[...]
                v = jnp.where(lane < 64, term(2 * q), other)
                rsend[2 * q] = v[0:32].astype(BF16)
                rsend[2 * q + 1] = v[32:64].astype(BF16)
            c0, n = (0, 8, 18)[a], (8, 10, 10)[a]

            @pl.loop(0, n)
            def _(k):
                m = c0 + lax.rem(me + k, n)
                pl.when(m != mine)(lambda: r1_send(m).start())

    def filler_one():
        each_snap(1, GY, lambda d, s: sn_send(d, s).start())
        for side, ok in x_sides:
            pl.when(ok)(lambda side=side: g_copy(side, True).start())
        for x in range(2):
            windows(x + 1, g[x])
            GT[x] = W[x + 1].T

    def filler_two():
        for side, ok in x_sides:
            pl.when(ok)(lambda side=side: g_copy(side, False).wait_recv())
        windows(0, grcv[0])
        windows(3, grcv[1])
        back(0)
        back(1)

    sweeps(RAD - 1, RAD)
    exchange(0, filler_one)
    sweeps(6, 7)
    exchange(1, filler_two)
    sweeps(6, 6)

    for side, ok in x_sides:
        pl.when(ok)(lambda side=side: fx_copy(side, False).wait_recv())
    for side, ok in y_sides:
        pl.when(ok)(lambda side=side: fy_copy(side, False).wait_recv())

    pool = jnp.where(iota((FZ, 128), 0) // 4 == iota((FZ, 128), 1), 1.0 / 64.0, 0.0).astype(BF16)
    row8 = iota((8, FZ), 0)
    sums = []
    total = None
    for x in range(8):
        pc = PP[x + 8]
        px = 0.5 * (PP[x + 9, 8:16] - PP[x + 7, 8:16])
        py = 0.5 * (pltpu.roll(pc, 23, 0) - pltpu.roll(pc, 1, 0))[8:16]
        pm = pc[8:16]
        pz = 0.5 * (z_after(pm, 1) - z_before(pm, 1))
        fm = lev[x]
        f_lo = fxr[0] if x == 0 else lev[x - 1]
        f_hi = fxr[1] if x == 7 else lev[x + 1]
        fx = 0.5 * (f_hi - f_lo)
        y_lo = jnp.where(row8 == 0, fyr[0, x : x + 1, :], pltpu.roll(fm, 1, 0))
        y_hi = jnp.where(row8 == 7, fyr[1, x : x + 1, :], pltpu.roll(fm, 7, 0))
        fy = 0.5 * (y_hi - y_lo)
        fz = 0.5 * (z_after(fm, 1) - z_before(fm, 1))
        new = fm + 2.0 * (px * fx + py * fy + pz * fz)
        newl[x] = new
        prs[x] = pm
        total = new if x % 4 == 0 else total + new
        if x % 4 == 3:
            t = total + pltpu.roll(total, 7, 0)
            sums.append(t + pltpu.roll(t, 6, 0))
    rest, mean = jnp.concatenate(sums, axis=0), 0.0
    for _ in range(3):
        part = rest.astype(BF16)
        rest = rest - part.astype(F32)
        mean = mean + dot(part, pool)
    for r in range(4):
        snsend[0, r : r + 1, :] = mean[4 * r : 4 * r + 1, :]
    snsend[0, 4:8, :] = jnp.zeros((4, 128), F32)

    each_snap(0, 1, lambda d, s: sn_send(d, s).start())
    stores = [
        pltpu.make_async_copy(a, b, out_s.at[k])
        for k, (a, b) in enumerate(
            ((newl, newl_h), (prs, prs_h), (r3, sum_h))
        )
    ]
    stores[0].start()
    stores[1].start()
    layers()

    for d in range(8):
        @pl.when(has(d))
        def _():
            ab_copy(d, True).wait_send()
            p_copy(0, d, True).wait_send()
            p_copy(1, d, True).wait_send()

    for side, ok in x_sides:
        @pl.when(ok)
        def _():
            fx_copy(side, True).wait_send()
            g_copy(side, True).wait_send()

    for side, ok in y_sides:
        pl.when(ok)(lambda side=side: fy_copy(side, True).wait_send())
    each_snap(0, GY, lambda d, s: sn_send(d, s).wait_send())

    @pl.when(mine < CHUNKS)
    def _():
        def add(k, total):
            m = lax.rem(me + k, GROUP)
            r1_recv(m).wait_recv()
            return total + r1[m].astype(F32)

        r2[mez] = lax.fori_loop(1, GROUP, add, rsend[mine].astype(F32))

        @pl.loop(1, ZS)
        def _(k):
            r2_copy(lax.rem(mez + k, ZS), mez).start()

        @pl.loop(1, ZS)
        def _(k):
            m = lax.rem(mez + k, ZS)
            r2_copy(m, m).wait_recv()

        total = r2[0]
        for k in range(1, ZS):
            total = total + r2[k]
        f3[...] = total.astype(BF16)

        @pl.loop(1, GROUP)
        def _(k):
            r3_copy(lax.rem(me + k, GROUP), mine).start()

        r3[mine] = f3[...]

    @pl.loop(0, CHUNKS)
    def _(m):
        pl.when(m != mine)(lambda: r1_send(m).wait_send())

    @pl.when(mine < CHUNKS)
    def _():
        @pl.loop(1, ZS)
        def _(k):
            r2_copy(lax.rem(mez + k, ZS), mez).wait_send()

    @pl.loop(0, CHUNKS)
    def _(m):
        pl.when(m != mine)(lambda: r3_copy(m, m).wait_recv())

    stores[2].start()

    @pl.when(mine < CHUNKS)
    def _():
        @pl.loop(1, GROUP)
        def _(k):
            r3_copy(lax.rem(me + k, GROUP), mine).wait_send()

    for c in stores:
        c.wait()


def leave(
    newl_h, prs_h, sum_h, newl_o, prs_o, dw1_o, dw2_o,
    newl, prs, total, dw1, dw2, in_s, out_s,
):
    ins = [
        pltpu.make_async_copy(a, b, in_s.at[k])
        for k, (a, b) in enumerate(((sum_h, total), (newl_h, newl), (prs_h, prs)))
    ]
    outs = [
        pltpu.make_async_copy(a, b, out_s.at[k])
        for k, (a, b) in enumerate(
            ((newl, newl_o), (prs, prs_o), (dw1, dw1_o), (dw2, dw2_o))
        )
    ]
    for c in ins:
        c.start()
    ins[0].wait()
    for q in range(14):
        v = jnp.concatenate([total[2 * q], total[2 * q + 1]], axis=0).astype(F32)
        if q < 13:
            dw2[:, 128 * q : 128 * q + 128] = v
        else:
            dw2[:, 128 * q : 128 * q + 64] = v[:, 0:64]
            dw1[...] = pltpu.roll(v, 64, 1)[0:27, 0:64]
    outs[3].start()
    outs[2].start()
    ins[1].wait()
    outs[0].start()
    ins[2].wait()
    outs[1].start()
    for c in outs:
        c.wait()


def per_device(
    level_set, source, stiffness, snap_buffer, buffer_order, first_weight, second_weight, out_grad
):
    snap = snap_buffer.reshape(8, 4, 64)
    g = out_grad.reshape(2, 16, 4096)
    vm = pl.BlockSpec(memory_space=pltpu.VMEM)
    sm = pl.BlockSpec(memory_space=pltpu.SMEM)
    hbm = pl.BlockSpec(memory_space=pltpu.HBM)
    dma = pltpu.SemaphoreType.DMA
    shapes = (
        jax.ShapeDtypeStruct((8, 8, FZ), F32),
        jax.ShapeDtypeStruct((8, 8, FZ), F32),
        jax.ShapeDtypeStruct((27, 64), F32),
        jax.ShapeDtypeStruct((64, 1728), F32),
    )
    sums = jax.ShapeDtypeStruct((CHUNKS, 32, 128), BF16)
    results = pl.pallas_call(
        kernel,
        out_shape=shapes[:2] + (sums,),
        in_specs=[hbm, hbm, hbm, vm, sm, vm, hbm, hbm],
        out_specs=(hbm,) * 3,
        scratch_shapes=[
            pltpu.VMEM((8, 8, FZ), F32),
            pltpu.VMEM((8, 8, FZ), F32),
            dma((3,)),
            pltpu.VMEM((8, 8, FZ), F32),
            pltpu.VMEM((8, 8, FZ), F32),
            pltpu.VMEM((8, 8, FZ), F32),
            pltpu.VMEM((64, 1728), BF16),
            pltpu.VMEM((2, 16, 4096), BF16),
            pltpu.VMEM((64, 1792), F32),
            dma((5,)),
            pltpu.VMEM((24, 24, FZ), F32),
            pltpu.VMEM((24, 24, FZ), F32),
            pltpu.VMEM((24, 24, FZ), F32),
            pltpu.VMEM((8, 16, FZ), BF16),
            pltpu.VMEM((8, 8, 16, FZ), BF16),
            pltpu.VMEM((2, 4, 16, FZ), BF16),
            pltpu.VMEM((2, 8, 4, 16, FZ), BF16),
            pltpu.VMEM((2, 8, FZ), F32),
            pltpu.VMEM((2, 8, FZ), F32),
            pltpu.VMEM((2, 8, FZ), F32),
            pltpu.VMEM((8, 8, 128), F32),
            pltpu.VMEM((3, 8, 8, 128), F32),
            pltpu.VMEM((2, 16, 4096), BF16),
            pltpu.VMEM((4, ROWS, 256), BF16),
            pltpu.VMEM((2, 256, ROWS), BF16),
            pltpu.VMEM((3, 256, 384), BF16),
            pltpu.VMEM((2, 256, 384), BF16),
            pltpu.VMEM((32, 128), F32),
            pltpu.VMEM((6, 16, 128), F32),
            pltpu.VMEM((4, 16, 256), F32),
            pltpu.VMEM((4, ROWS, 384), BF16),
            pltpu.VMEM((2, ROWS, 384), BF16),
            pltpu.VMEM((2, 256, ROWS), BF16),
            pltpu.VMEM((2, ROWS, 128), F32),
            pltpu.VMEM((3, 256, 384), F32),
            pltpu.VMEM((64, 128), F32),
            pltpu.VMEM((CHUNKS, 32, 128), BF16),
            pltpu.VMEM((GROUP, 32, 128), BF16),
            pltpu.VMEM((ZS, 32, 128), F32),
            pltpu.VMEM((32, 128), BF16),
            pltpu.VMEM((CHUNKS, 32, 128), BF16),
            dma((8,)), dma((8,)), dma((2, 8)), dma((2, 8)), dma((4,)), dma((4,)),
            dma((3, 8)), dma((3, 8)), dma((2,)), dma((2,)),
            dma((CHUNKS,)), dma((GROUP,)), dma((ZS,)), dma((ZS,)), dma((GROUP,)), dma((CHUNKS,)),
        ],
        compiler_params=pltpu.CompilerParams(
            collective_id=0, has_side_effects=True, vmem_limit_bytes=60 * 1024 * 1024
        ),
    )(source, stiffness, level_set, snap, buffer_order, first_weight, second_weight.T, g)
    results = pl.pallas_call(
        leave,
        out_shape=shapes,
        in_specs=[hbm] * 3,
        out_specs=(hbm,) * 4,
        scratch_shapes=[
            pltpu.VMEM(shapes[0].shape, F32),
            pltpu.VMEM(shapes[1].shape, F32),
            pltpu.VMEM(sums.shape, BF16),
            pltpu.VMEM(shapes[2].shape, F32),
            pltpu.VMEM(shapes[3].shape, F32),
            dma((3,)),
            dma((4,)),
        ],
        compiler_params=pltpu.CompilerParams(vmem_limit_bytes=60 * 1024 * 1024),
    )(*results)
    return results[0], results[1], results[2], results[3].T


def solution(mesh):
    placed = (
        P("gx", "gy", None),
        P("gx", "gy", None),
        P("gx", "gy", None),
        P(None, "gx", "gy", None),
        P(),
        P(),
        P(),
        P("gy", "gx", None, None),
    )
    return jax.shard_map(
        per_device,
        mesh=mesh,
        in_specs=placed,
        out_specs=(P("gx", "gy", None), P("gx", "gy", None), P(), P()),
        check_vma=False,
    )
```

```python
import functools

import jax
import jax.numpy as jnp
from jax import lax
from jax.experimental import pallas as pl
from jax.experimental.pallas import tpu as pltpu
from jax.sharding import PartitionSpec as P

F32 = jnp.float32
BF16 = jnp.bfloat16
MESH = pl.DeviceIdType.MESH
GX, GY = 32, 8
FZ = 256
T = 8
ROWS = 512
RAD = 6
GROUP = 32
CHUNKS = 28
ZS = 8
DIRS = [(dx, dy) for dx in (-1, 0, 1) for dy in (-1, 0, 1) if (dx, dy) != (0, 0)]

FAR_FIRST = (0, 2, 5, 7, 1, 6, 3, 4)
NEAR_FIRST = FAR_FIRST[::-1]


def dot(a, b, dims=((1,), (0,)), precision=None):
    return lax.dot_general(
        a, b, (dims, ((), ())), preferred_element_type=F32, precision=precision
    )


def iota(shape, dim):
    return lax.broadcasted_iota(jnp.int32, shape, dim)


def tile_rows(dx, n):
    return {-1: (T - n, n), 0: (0, T), 1: (0, n)}[dx]


def row_before(v):
    y = iota(v.shape, 0) & 15
    return jnp.where(y == 0, 0.0, pltpu.roll(v, 1, 0))


def row_after(v):
    y = iota(v.shape, 0) & 15
    return jnp.where(y == 15, 0.0, pltpu.roll(v, v.shape[0] - 1, 0))


def z_before(v, axis):
    z = iota(v.shape, axis)
    return jnp.where(z == 0, 0.0, pltpu.roll(v, 1, axis))


def z_after(v, axis):
    z = iota(v.shape, axis)
    return jnp.where(z == FZ - 1, 0.0, pltpu.roll(v, FZ - 1, axis))


def kernel(
    src_h, stf_h, lev_h, snp_h, order, w1_h, w2_h, g_h,
    newl_h, prs_h, sum_h,
    newl, prs, out_s,
    src, stf, lev, w2, g, snp, w1, w2p, in_s,
    A, B, PP, absend, abrcv, psend, prcv, fysend, fxr, fyr,
    snsend, snrcv, grcv, W, GT, BT, V, w1s, S6, CC, H3, DZ3, LT, dh, acc, d1,
    rsend, r1, r2, f3, r3,
    ab_ss, ab_rs, p_ss, p_rs, f_ss, f_rs, sn_ss, sn_rs, g_ss, g_rs,
    r1_ss, r1_rs, r2_ss, r2_rs, r3_ss, r3_rs,
):
    i = lax.axis_index("gx")
    j = lax.axis_index("gy")
    has_l, has_r = i > 0, i < GX - 1
    has_x = {-1: has_l, 0: True, 1: has_r}
    has_y = {-1: j > 0, 0: True, 1: j < GY - 1}

    def has(d):
        dx, dy = DIRS[d]
        if dx == 0:
            return has_y[dy]
        if dy == 0:
            return has_x[dx]
        return jnp.logical_and(has_x[dx], has_y[dy])

    cy, czh, cc = i // 8, (i // 2) % 4, i % 2
    czl, cx = j // 4, j % 4
    me = cy * 8 + cc * 4 + cx
    mez = czh * 2 + czl
    mine = lax.rem(3 * me, GROUP)

    def member(m):
        return ((m // 8) * 8 + czh * 2 + (m // 4) % 2, czl * 4 + m % 4)

    def zpeer(k):
        return (cy * 8 + (k // 2) * 2 + cc, (k % 2) * 4 + cx)

    loads = [
        pltpu.make_async_copy(a, b, in_s.at[k])
        for k, (a, b) in enumerate(
            (
                (src_h, src), (stf_h, stf), (lev_h, lev), (g_h, g), (w2_h, w2),
                (snp_h, snp), (w1_h, w1),
            )
        )
    ]
    for c in loads:
        c.start()

    bar = pltpu.get_barrier_semaphore()

    def greet(dev):
        pl.semaphore_signal(bar, inc=1, device_id=dev, device_id_type=MESH)

    @pl.loop(1, ZS)
    def _(k):
        greet(zpeer(lax.rem(mez + k, ZS)))

    @pl.loop(1, GROUP)
    def _(k):
        greet(member(lax.rem(me + k, GROUP)))

    @pl.when(has_l)
    def _():
        @pl.loop(0, GY)
        def _(s):
            greet((i - 1, s))

    @pl.when(has_r)
    def _():
        @pl.loop(0, GY)
        def _(s):
            greet((i + 1, s))

    @pl.loop(1, GY)
    def _(k):
        greet((i, lax.rem(j + k, GY)))

    for c in loads[:4]:
        c.wait()
    a_own = 1.0 / (6.0 + stf[...])
    b_own = src[...] * a_own
    A[8:16, 8:16, :] = a_own
    B[8:16, 8:16, :] = b_own
    PP[8:16, 8:16, :] = b_own
    absend[...] = jnp.concatenate([a_own, b_own], axis=1).astype(BF16)
    fysend[0] = lev[:, 0, :]
    fysend[1] = lev[:, 7, :]
    zero_tile = jnp.zeros((T, T, FZ), F32)
    for d, (dx, dy) in enumerate(DIRS):
        xs, ys = pl.ds(8 + 8 * dx, 8), pl.ds(8 + 8 * dy, 8)

        @pl.when(jnp.logical_not(has(d)))
        def _():
            A[xs, ys, :] = zero_tile
            B[xs, ys, :] = zero_tile
            PP[xs, ys, :] = zero_tile

    @pl.when(jnp.logical_not(has_l))
    def _():
        fxr[0] = jnp.zeros((T, FZ), F32)
        snrcv[0] = jnp.zeros((GY, 8, 128), F32)
        grcv[0] = jnp.zeros((16, 4096), BF16)

    @pl.when(jnp.logical_not(has_r))
    def _():
        fxr[1] = jnp.zeros((T, FZ), F32)
        snrcv[2] = jnp.zeros((GY, 8, 128), F32)
        grcv[1] = jnp.zeros((16, 4096), BF16)

    @pl.when(j == 0)
    def _():
        fyr[0] = jnp.zeros((T, FZ), F32)

    @pl.when(j == GY - 1)
    def _():
        fyr[1] = jnp.zeros((T, FZ), F32)

    loads[5].wait()
    snsend[...] = jnp.zeros((8, 8, 128), F32)
    for s in range(1, 8):
        snsend[s, 0:4, 0:64] = snp[order[s]].astype(F32)

    n_bar = (GY - 1) + (GROUP - 1) + (ZS - 1)
    n_bar = n_bar + jnp.where(has_l, GY, 0) + jnp.where(has_r, GY, 0)
    pl.semaphore_wait(bar, n_bar)

    def ab_copy(d, to):
        dx, dy = DIRS[d]
        slot = 7 - d if to else d
        send_dx = dx if to else -dx
        lo, n = tile_rows(-send_dx, RAD if dy == 0 else RAD - 1)
        rows = pl.ds(lo, n)
        return pltpu.make_async_remote_copy(
            src_ref=absend.at[rows], dst_ref=abrcv.at[slot, rows],
            send_sem=ab_ss.at[d], recv_sem=ab_rs.at[slot],
            device_id=(i + dx, j + dy), device_id_type=MESH,
        )

    def p_copy(e, d, to):
        dx, dy = DIRS[d]
        slot = 7 - d if to else d
        lo, n = tile_rows(-dx if to else dx, 8 if dy == 0 else 6)
        rows = pl.ds(lo // 2, n // 2)
        return pltpu.make_async_remote_copy(
            src_ref=psend.at[e, rows], dst_ref=prcv.at[e, slot, rows],
            send_sem=p_ss.at[e, d], recv_sem=p_rs.at[e, slot],
            device_id=(i + dx, j + dy), device_id_type=MESH,
        )

    def fx_copy(side, to):
        slot = 1 - side if to else side
        return pltpu.make_async_remote_copy(
            src_ref=lev.at[0 if side == 0 else 7], dst_ref=fxr.at[slot],
            send_sem=f_ss.at[side], recv_sem=f_rs.at[slot],
            device_id=(i + (2 * side - 1), j), device_id_type=MESH,
        )

    def fy_copy(side, to):
        slot = 1 - side if to else side
        return pltpu.make_async_remote_copy(
            src_ref=fysend.at[side], dst_ref=fyr.at[slot],
            send_sem=f_ss.at[2 + side], recv_sem=f_rs.at[2 + slot],
            device_id=(i, j + (2 * side - 1)), device_id_type=MESH,
        )

    def g_copy(side, to):
        slot = 1 - side if to else side
        return pltpu.make_async_remote_copy(
            src_ref=g.at[side], dst_ref=grcv.at[slot],
            send_sem=g_ss.at[side], recv_sem=g_rs.at[slot],
            device_id=(i + (2 * side - 1), j), device_id_type=MESH,
        )

    def sn_send(d, s):
        return pltpu.make_async_remote_copy(
            src_ref=snsend.at[s], dst_ref=snrcv.at[1 - d, j],
            send_sem=sn_ss.at[d + 1, s], recv_sem=sn_rs.at[1 - d, j],
            device_id=(i + d, s), device_id_type=MESH,
        )

    def sn_recv(d, y):
        return pltpu.make_async_remote_copy(
            src_ref=snsend.at[0], dst_ref=snrcv.at[d + 1, y],
            send_sem=sn_ss.at[d + 1, 0], recv_sem=sn_rs.at[d + 1, y],
            device_id=(i, j), device_id_type=MESH,
        )

    x_sides = ((0, has_l), (1, has_r))
    y_sides = ((0, has_y[-1]), (1, has_y[1]))

    for d in FAR_FIRST:
        pl.when(has(d))(lambda d=d: ab_copy(d, True).start())
    for side, ok in x_sides:
        pl.when(ok)(lambda side=side: fx_copy(side, True).start())
    for side, ok in y_sides:
        pl.when(ok)(lambda side=side: fy_copy(side, True).start())
    def each_snap(lo, hi, act):
        @pl.loop(lo, hi)
        def _(s):
            pl.when(has_l)(lambda: act(-1, s))
            pl.when(s != j)(lambda: act(0, s))
            pl.when(has_r)(lambda: act(1, s))


    loads[4].wait()
    w2p[:, 0:1728] = w2[...].astype(F32)
    even = w2p[...]
    odd = pltpu.roll(even, 64, 1)
    left = iota((64, 128), 1) < 64

    def pair(o):
        t = ((o + 1) // 2) * 128
        return (odd if o % 2 else even)[:, t : t + 128]

    for a in range(3):
        for b in range(3):
            o = 9 * a + 3 * b
            tiles = (
                jnp.where(left, pair(o + 2), 0.0),
                pair(o + 1),
                pair(o),
                jnp.where(left, 0.0, pair(o - 1)),
            )
            for k, v in enumerate(tiles):
                BT[a, 64 * k : 64 * k + 64, 128 * b : 128 * b + 128] = v.astype(BF16)

    loads[6].wait()
    w1s[...] = jnp.zeros((32, 128), F32)
    w1s[0:27, 0:64] = w1[...].astype(F32)
    w1d = w1s[...]
    w1d = jnp.concatenate([w1d, pltpu.roll(w1d, 64, 1)], axis=0).astype(BF16)
    for par in range(2):
        for b in range(3):
            k = iota((256, 64), 0)
            col = iota((256, 64), 1)
            zo = col // 32
            zi = ((k & 63) + 5 - 2 * par) & 3
            cz = zi - zo
            want = 9 * (k // 64) + 3 * b + cz
            hit = (col % 32 == want) & (cz >= 0) & (cz < 3) & (k < 192)
            V[par, :, b * 128 : (b + 1) * 128] = dot(
                jnp.where(hit, 1.0, 0.0).astype(BF16), w1d
            ).astype(BF16)

    lane128 = iota((16, 128), 1)

    def windows(plane, gv):
        gr = pltpu.roll(gv.astype(F32), 64, 1)
        for t in range(33):
            if t == 0:
                tile = jnp.where(lane128 >= 64, gr[:, 0:128], 0.0)
            elif t == 32:
                tile = jnp.where(lane128 < 64, gr[:, 0:128], 0.0)
            else:
                tile = gr[:, 128 * t : 128 * (t + 1)]
            tile = tile.astype(BF16)
            if t < 32:
                r = ((t % 2) * 16 + t // 2) * 16
                W[plane, r : r + 16, 0:128] = tile
            if t > 0:
                r = (((t - 1) % 2) * 16 + (t - 1) // 2) * 16
                W[plane, r : r + 16, 128:256] = tile

    for d in NEAR_FIRST:
        dx, dy = DIRS[d]
        lo, n = tile_rows(dx, RAD if dy == 0 else RAD - 1)
        xs, ys = pl.ds(8 + 8 * dx + lo, n), pl.ds(8 + 8 * dy, 8)

        @pl.when(has(d))
        def _():
            ab_copy(d, False).wait_recv()
            v = abrcv[d, lo : lo + n].astype(F32)
            A[xs, ys, :] = v[:, 0:8]
            B[xs, ys, :] = v[:, 8:16]
            PP[xs, ys, :] = v[:, 8:16]

    def around(v):
        rows = pltpu.roll(v, 1, 0) + pltpu.roll(v, 23, 0)
        return rows + z_before(v, 1) + z_after(v, 1)

    def sweeps(first, count):
        for rad in range(first, first - count, -1):
            lo, hi = 8 - rad, 16 + rad
            before, cur = PP[lo - 1], PP[lo]
            for x in range(lo, hi):
                after = PP[x + 1]
                PP[x] = B[x] + A[x] * (before + after + around(cur))
                before, cur = cur, after

    def exchange(e, filler):
        own = PP[8:16, 8:16, :]
        psend[e] = own.reshape(4, 16, FZ).astype(BF16)
        for d in FAR_FIRST:
            pl.when(has(d))(lambda d=d: p_copy(e, d, True).start())
        filler()
        for d in NEAR_FIRST:
            dx, dy = DIRS[d]
            lo, n = tile_rows(dx, 8 if dy == 0 else 6)
            xs, ys = pl.ds(8 + 8 * dx + lo, n), pl.ds(8 + 8 * dy, 8)

            @pl.when(has(d))
            def _():
                p_copy(e, d, False).wait_recv()
                v = prcv[e, d, lo // 2 : (lo + n) // 2].astype(F32)
                PP[xs, ys, :] = v.reshape(n, 8, FZ)

    def back(x):
        @pl.loop(0, 4)
        def _(q):
            rows = pl.ds(pl.multiple_of(q * 128, 128), 128)
            r = dot(W[x + 2, rows, :], BT[0])
            r = r + dot(W[x + 1, rows, :], BT[1])
            r = r + dot(W[x, rows, :], BT[2])
            dh[x, rows, :] = (
                row_after(r[:, 0:128]) + r[:, 128:256] + row_before(r[:, 256:384])
            )

    lane = iota((64, 128), 1)

    def term(o):
        a, b, c = o // 9, (o // 3) % 3, o % 3
        r = (2 - c) * 64
        cols = slice(b * 128, b * 128 + 128)
        v = jnp.where(lane < 64, acc[a, r : r + 64, cols], acc[a, r + 64 : r + 128, cols])
        return v + pltpu.roll(v, 64, 1)

    def r1_send(m):
        return pltpu.make_async_remote_copy(
            src_ref=rsend.at[m], dst_ref=r1.at[me],
            send_sem=r1_ss.at[m], recv_sem=r1_rs.at[me],
            device_id=member(lax.rem(11 * m, GROUP)), device_id_type=MESH,
        )

    def r1_recv(m):
        return pltpu.make_async_remote_copy(
            src_ref=rsend.at[0], dst_ref=r1.at[m],
            send_sem=r1_ss.at[0], recv_sem=r1_rs.at[m],
            device_id=member(m), device_id_type=MESH,
        )

    def r2_copy(k, slot):
        return pltpu.make_async_remote_copy(
            src_ref=r2.at[mez], dst_ref=r2.at[slot],
            send_sem=r2_ss.at[k], recv_sem=r2_rs.at[slot],
            device_id=zpeer(k), device_id_type=MESH,
        )

    def r3_copy(m, slot):
        return pltpu.make_async_remote_copy(
            src_ref=f3, dst_ref=r3.at[slot],
            send_sem=r3_ss.at[m], recv_sem=r3_rs.at[slot],
            device_id=member(m), device_id_type=MESH,
        )

    def first_gradient():
        spread = jnp.where((iota((16, ROWS), 1) & 15) == iota((16, ROWS), 0), 1.0, 0.0).astype(BF16)
        r_k = iota((256, ROWS), 0) & 63
        r_c = iota((256, ROWS), 1)
        jj = 2 * ((r_c & 255) // 16) + r_c // 256
        t = r_k - 2 * jj + 1
        near = (t >= 0) & (t < 4)
        for x in range(2):
            LT[x] = jnp.where(near, dot(CC[x + 1].T.astype(BF16), spread), 0.0).astype(BF16)
        parts = []
        for par in range(2):
            cols = slice(par * 256, par * 256 + 256)
            q = dot(LT[0, :, cols], DZ3[0, cols, :]) + dot(LT[1, :, cols], DZ3[1, cols, :])
            q = q.reshape(4, 8, 8, 384)
            parts.append([q[a].sum(0) for a in range(3)])
        d1[...] = jnp.zeros((64, 128), F32)
        for a in range(3):
            u, w = parts[0][a], parts[1][a]
            u = u + pltpu.roll(u, 4, 0)
            w = w + pltpu.roll(w, 4, 0)
            u = u + pltpu.roll(w, 2, 0)
            for b in range(3):
                v = u[:, b * 128 : (b + 1) * 128]
                v = pltpu.roll(v, 64, 1) + pltpu.roll(v, 7, 0)
                v = pltpu.roll(v, 1, 0)
                d1[9 * a + 3 * b : 9 * a + 3 * b + 3, :] = v[0:3]

    def layers():
        snrcv[1, j] = snsend[j]
        @pl.when(has_l)
        def _():
            @pl.loop(0, GY)
            def _(y):
                sn_recv(-1, y).wait_recv()

        @pl.when(has_r)
        def _():
            @pl.loop(0, GY)
            def _(y):
                sn_recv(1, y).wait_recv()

        @pl.loop(1, GY)
        def _(k):
            sn_recv(0, lax.rem(j + k, GY)).wait_recv()

        for d in range(3):
            for y in range(8):
                t = snrcv[d, y]
                S6[2 * d, 2 * y : 2 * y + 2, :] = t[0:2]
                S6[2 * d + 1, 2 * y : 2 * y + 2, :] = t[2:4]
        for p in range(4):
            CC[p, :, 0:128] = S6[p] + pltpu.roll(S6[p + 1], 64, 1)
            CC[p, :, 128:256] = S6[p + 2]

        for p in range(4):
            keep = {0: jnp.where(has_l, 1.0, 0.0), 3: jnp.where(has_r, 1.0, 0.0)}.get(p)

            for q in range(4):
                rows = slice(q * 128, q * 128 + 128)
                par = q // 2
                jj = 2 * ((q % 2) * 8 + iota((8, 16, 256), 0)) + par
                t = (iota((8, 16, 256), 2) & 63) - 2 * jj + 1
                mask = (t >= 0) & (t < 4)
                v = jnp.broadcast_to(CC[p][None], (8, 16, 256))
                v = jnp.where(mask, v, 0.0).reshape(128, 256).astype(BF16)
                r = dot(v, V[par])
                z = row_before(r[:, 0:128]) + r[:, 128:256] + row_after(r[:, 256:384])
                sig = 1.0 / (1.0 + jnp.exp(-z))
                h = z * sig
                if keep is not None:
                    h = h * keep
                H3[p, rows, 0:128] = row_before(h).astype(BF16)
                H3[p, rows, 128:256] = h.astype(BF16)
                H3[p, rows, 256:384] = row_after(h).astype(BF16)
                if p in (1, 2):
                    dz = dh[p - 1, rows, :] * (sig * (1.0 + z * (1.0 - sig)))
                    DZ3[p - 1, rows, 0:128] = row_after(dz).astype(BF16)
                    DZ3[p - 1, rows, 128:256] = dz.astype(BF16)
                    DZ3[p - 1, rows, 256:384] = row_before(dz).astype(BF16)

        for a in range(3):
            acc[a] = dot(GT[0], H3[a]) + dot(GT[1], H3[a + 1])
            if a == 2:
                first_gradient()
            for q in range((0, 4, 9)[a], (4, 9, 14)[a]):
                other = term(2 * q + 1) if q < 13 else d1[...]
                v = jnp.where(lane < 64, term(2 * q), other)
                rsend[2 * q] = v[0:32].astype(BF16)
                rsend[2 * q + 1] = v[32:64].astype(BF16)
            c0, n = (0, 8, 18)[a], (8, 10, 10)[a]

            @pl.loop(0, n)
            def _(k):
                m = c0 + lax.rem(me + k, n)
                pl.when(m != mine)(lambda: r1_send(m).start())

    def filler_one():
        each_snap(1, GY, lambda d, s: sn_send(d, s).start())
        for side, ok in x_sides:
            pl.when(ok)(lambda side=side: g_copy(side, True).start())
        for x in range(2):
            windows(x + 1, g[x])
            GT[x] = W[x + 1].T

    def filler_two():
        for side, ok in x_sides:
            pl.when(ok)(lambda side=side: g_copy(side, False).wait_recv())
        windows(0, grcv[0])
        windows(3, grcv[1])
        back(0)
        back(1)

    sweeps(RAD - 1, RAD)
    exchange(0, filler_one)
    sweeps(6, 7)
    exchange(1, filler_two)
    sweeps(6, 6)

    for side, ok in x_sides:
        pl.when(ok)(lambda side=side: fx_copy(side, False).wait_recv())
    for side, ok in y_sides:
        pl.when(ok)(lambda side=side: fy_copy(side, False).wait_recv())

    pool = jnp.where(iota((FZ, 128), 0) // 4 == iota((FZ, 128), 1), 1.0 / 64.0, 0.0).astype(BF16)
    row8 = iota((8, FZ), 0)
    sums = []
    total = None
    for x in range(8):
        pc = PP[x + 8]
        px = 0.5 * (PP[x + 9, 8:16] - PP[x + 7, 8:16])
        py = 0.5 * (pltpu.roll(pc, 23, 0) - pltpu.roll(pc, 1, 0))[8:16]
        pm = pc[8:16]
        pz = 0.5 * (z_after(pm, 1) - z_before(pm, 1))
        fm = lev[x]
        f_lo = fxr[0] if x == 0 else lev[x - 1]
        f_hi = fxr[1] if x == 7 else lev[x + 1]
        fx = 0.5 * (f_hi - f_lo)
        y_lo = jnp.where(row8 == 0, fyr[0, x : x + 1, :], pltpu.roll(fm, 1, 0))
        y_hi = jnp.where(row8 == 7, fyr[1, x : x + 1, :], pltpu.roll(fm, 7, 0))
        fy = 0.5 * (y_hi - y_lo)
        fz = 0.5 * (z_after(fm, 1) - z_before(fm, 1))
        new = fm + 2.0 * (px * fx + py * fy + pz * fz)
        newl[x] = new
        prs[x] = pm
        total = new if x % 4 == 0 else total + new
        if x % 4 == 3:
            t = total + pltpu.roll(total, 7, 0)
            sums.append(t + pltpu.roll(t, 6, 0))
    rest, mean = jnp.concatenate(sums, axis=0), 0.0
    for _ in range(3):
        part = rest.astype(BF16)
        rest = rest - part.astype(F32)
        mean = mean + dot(part, pool)
    for r in range(4):
        snsend[0, r : r + 1, :] = mean[4 * r : 4 * r + 1, :]
    snsend[0, 4:8, :] = jnp.zeros((4, 128), F32)

    each_snap(0, 1, lambda d, s: sn_send(d, s).start())
    stores = [
        pltpu.make_async_copy(a, b, out_s.at[k])
        for k, (a, b) in enumerate(
            ((newl, newl_h), (prs, prs_h), (r3, sum_h))
        )
    ]
    stores[0].start()
    stores[1].start()
    layers()

    for d in range(8):
        @pl.when(has(d))
        def _():
            ab_copy(d, True).wait_send()
            p_copy(0, d, True).wait_send()
            p_copy(1, d, True).wait_send()

    for side, ok in x_sides:
        @pl.when(ok)
        def _():
            fx_copy(side, True).wait_send()
            g_copy(side, True).wait_send()

    for side, ok in y_sides:
        pl.when(ok)(lambda side=side: fy_copy(side, True).wait_send())
    each_snap(0, GY, lambda d, s: sn_send(d, s).wait_send())

    @pl.when(mine < CHUNKS)
    def _():
        def add(k, total):
            m = lax.rem(me + k, GROUP)
            r1_recv(m).wait_recv()
            return total + r1[m].astype(F32)

        r2[mez] = lax.fori_loop(1, GROUP, add, rsend[mine].astype(F32))

        @pl.loop(1, ZS)
        def _(k):
            r2_copy(lax.rem(mez + k, ZS), mez).start()

        @pl.loop(1, ZS)
        def _(k):
            m = lax.rem(mez + k, ZS)
            r2_copy(m, m).wait_recv()

        total = r2[0]
        for k in range(1, ZS):
            total = total + r2[k]
        f3[...] = total.astype(BF16)

        @pl.loop(1, GROUP)
        def _(k):
            r3_copy(lax.rem(me + k, GROUP), mine).start()

        r3[mine] = f3[...]

    @pl.loop(0, CHUNKS)
    def _(m):
        pl.when(m != mine)(lambda: r1_send(m).wait_send())

    @pl.when(mine < CHUNKS)
    def _():
        @pl.loop(1, ZS)
        def _(k):
            r2_copy(lax.rem(mez + k, ZS), mez).wait_send()

    @pl.loop(0, CHUNKS)
    def _(m):
        pl.when(m != mine)(lambda: r3_copy(m, m).wait_recv())

    stores[2].start()

    @pl.when(mine < CHUNKS)
    def _():
        @pl.loop(1, GROUP)
        def _(k):
            r3_copy(lax.rem(me + k, GROUP), mine).wait_send()

    for c in stores:
        c.wait()


def leave(
    newl_h, prs_h, sum_h, newl_o, prs_o, dw1_o, dw2_o,
    newl, prs, total, dw1, dw2, in_s, out_s,
):
    ins = [
        pltpu.make_async_copy(a, b, in_s.at[k])
        for k, (a, b) in enumerate(((sum_h, total), (newl_h, newl), (prs_h, prs)))
    ]
    outs = [
        pltpu.make_async_copy(a, b, out_s.at[k])
        for k, (a, b) in enumerate(
            ((newl, newl_o), (prs, prs_o), (dw1, dw1_o), (dw2, dw2_o))
        )
    ]
    for c in ins:
        c.start()
    ins[0].wait()
    for q in range(14):
        v = jnp.concatenate([total[2 * q], total[2 * q + 1]], axis=0).astype(F32)
        if q < 13:
            dw2[:, 128 * q : 128 * q + 128] = v
        else:
            dw2[:, 128 * q : 128 * q + 64] = v[:, 0:64]
            dw1[...] = pltpu.roll(v, 64, 1)[0:27, 0:64]
    outs[3].start()
    outs[2].start()
    ins[1].wait()
    outs[0].start()
    ins[2].wait()
    outs[1].start()
    for c in outs:
        c.wait()


def per_device(
    level_set, source, stiffness, snap_buffer, buffer_order, first_weight, second_weight, out_grad
):
    snap = snap_buffer.reshape(8, 4, 64)
    g = out_grad.reshape(2, 16, 4096)
    sm = pl.BlockSpec(memory_space=pltpu.SMEM)
    hbm = pl.BlockSpec(memory_space=pltpu.HBM)
    dma = pltpu.SemaphoreType.DMA
    shapes = (
        jax.ShapeDtypeStruct((8, 8, FZ), F32),
        jax.ShapeDtypeStruct((8, 8, FZ), F32),
        jax.ShapeDtypeStruct((27, 64), F32),
        jax.ShapeDtypeStruct((64, 1728), F32),
    )
    sums = jax.ShapeDtypeStruct((CHUNKS, 32, 128), BF16)
    results = pl.pallas_call(
        kernel,
        out_shape=shapes[:2] + (sums,),
        in_specs=[hbm, hbm, hbm, hbm, sm, hbm, hbm, hbm],
        out_specs=(hbm,) * 3,
        scratch_shapes=[
            pltpu.VMEM((8, 8, FZ), F32),
            pltpu.VMEM((8, 8, FZ), F32),
            dma((3,)),
            pltpu.VMEM((8, 8, FZ), F32),
            pltpu.VMEM((8, 8, FZ), F32),
            pltpu.VMEM((8, 8, FZ), F32),
            pltpu.VMEM((64, 1728), BF16),
            pltpu.VMEM((2, 16, 4096), BF16),
            pltpu.VMEM((8, 4, 64), BF16),
            pltpu.VMEM((27, 64), BF16),
            pltpu.VMEM((64, 1792), F32),
            dma((7,)),
            pltpu.VMEM((24, 24, FZ), F32),
            pltpu.VMEM((24, 24, FZ), F32),
            pltpu.VMEM((24, 24, FZ), F32),
            pltpu.VMEM((8, 16, FZ), BF16),
            pltpu.VMEM((8, 8, 16, FZ), BF16),
            pltpu.VMEM((2, 4, 16, FZ), BF16),
            pltpu.VMEM((2, 8, 4, 16, FZ), BF16),
            pltpu.VMEM((2, 8, FZ), F32),
            pltpu.VMEM((2, 8, FZ), F32),
            pltpu.VMEM((2, 8, FZ), F32),
            pltpu.VMEM((8, 8, 128), F32),
            pltpu.VMEM((3, 8, 8, 128), F32),
            pltpu.VMEM((2, 16, 4096), BF16),
            pltpu.VMEM((4, ROWS, 256), BF16),
            pltpu.VMEM((2, 256, ROWS), BF16),
            pltpu.VMEM((3, 256, 384), BF16),
            pltpu.VMEM((2, 256, 384), BF16),
            pltpu.VMEM((32, 128), F32),
            pltpu.VMEM((6, 16, 128), F32),
            pltpu.VMEM((4, 16, 256), F32),
            pltpu.VMEM((4, ROWS, 384), BF16),
            pltpu.VMEM((2, ROWS, 384), BF16),
            pltpu.VMEM((2, 256, ROWS), BF16),
            pltpu.VMEM((2, ROWS, 128), F32),
            pltpu.VMEM((3, 256, 384), F32),
            pltpu.VMEM((64, 128), F32),
            pltpu.VMEM((CHUNKS, 32, 128), BF16),
            pltpu.VMEM((GROUP, 32, 128), BF16),
            pltpu.VMEM((ZS, 32, 128), F32),
            pltpu.VMEM((32, 128), BF16),
            pltpu.VMEM((CHUNKS, 32, 128), BF16),
            dma((8,)), dma((8,)), dma((2, 8)), dma((2, 8)), dma((4,)), dma((4,)),
            dma((3, 8)), dma((3, 8)), dma((2,)), dma((2,)),
            dma((CHUNKS,)), dma((GROUP,)), dma((ZS,)), dma((ZS,)), dma((GROUP,)), dma((CHUNKS,)),
        ],
        compiler_params=pltpu.CompilerParams(
            collective_id=0, has_side_effects=True, vmem_limit_bytes=60 * 1024 * 1024
        ),
    )(source, stiffness, level_set, snap, buffer_order, first_weight, second_weight.T, g)
    results = pl.pallas_call(
        leave,
        out_shape=shapes,
        in_specs=[hbm] * 3,
        out_specs=(hbm,) * 4,
        scratch_shapes=[
            pltpu.VMEM(shapes[0].shape, F32),
            pltpu.VMEM(shapes[1].shape, F32),
            pltpu.VMEM(sums.shape, BF16),
            pltpu.VMEM(shapes[2].shape, F32),
            pltpu.VMEM(shapes[3].shape, F32),
            dma((3,)),
            dma((4,)),
        ],
        compiler_params=pltpu.CompilerParams(vmem_limit_bytes=60 * 1024 * 1024),
    )(*results)
    return results[0], results[1], results[2], results[3].T


def solution(mesh):
    placed = (
        P("gx", "gy", None),
        P("gx", "gy", None),
        P("gx", "gy", None),
        P(None, "gx", "gy", None),
        P(),
        P(),
        P(),
        P("gy", "gx", None, None),
    )
    return jax.shard_map(
        per_device,
        mesh=mesh,
        in_specs=placed,
        out_specs=(P("gx", "gy", None), P("gx", "gy", None), P(), P()),
        check_vma=False,
    )
```

```python
import functools

import jax
import jax.numpy as jnp
from jax import lax
from jax.experimental import pallas as pl
from jax.experimental.pallas import tpu as pltpu
from jax.sharding import PartitionSpec as P

F32 = jnp.float32
BF16 = jnp.bfloat16
MESH = pl.DeviceIdType.MESH
GX, GY = 32, 8
FZ = 256
T = 8
ROWS = 512
RAD = 6
GROUP = 32
CHUNKS = 28
ZS = 8
DIRS = [(dx, dy) for dx in (-1, 0, 1) for dy in (-1, 0, 1) if (dx, dy) != (0, 0)]

FAR_FIRST = (0, 2, 5, 7, 1, 6, 3, 4)
NEAR_FIRST = FAR_FIRST[::-1]


def dot(a, b, dims=((1,), (0,)), precision=None):
    return lax.dot_general(
        a, b, (dims, ((), ())), preferred_element_type=F32, precision=precision
    )


def iota(shape, dim):
    return lax.broadcasted_iota(jnp.int32, shape, dim)


def tile_rows(dx, n):
    return {-1: (T - n, n), 0: (0, T), 1: (0, n)}[dx]


def row_before(v):
    y = iota(v.shape, 0) & 15
    return jnp.where(y == 0, 0.0, pltpu.roll(v, 1, 0))


def row_after(v):
    y = iota(v.shape, 0) & 15
    return jnp.where(y == 15, 0.0, pltpu.roll(v, v.shape[0] - 1, 0))


def z_before(v, axis):
    z = iota(v.shape, axis)
    return jnp.where(z == 0, 0.0, pltpu.roll(v, 1, axis))


def z_after(v, axis):
    z = iota(v.shape, axis)
    return jnp.where(z == FZ - 1, 0.0, pltpu.roll(v, FZ - 1, axis))


def kernel(
    src_h, stf_h, lev_h, snp_h, order, w1_h, w2_h, g_h,
    newl_h, prs_h, sum_h,
    newl, prs, out_s,
    src, stf, lev, w2, g, snp, w1, w2p, in_s,
    A, B, PP, absend, abrcv, psend, prcv, fysend, fxr, fyr,
    snsend, snrcv, grcv, W, GT, BT, V, w1s, S6, CC, H3, DZ3, LT, dh, acc, d1,
    rsend, r1, r2, f3, r3,
    ab_ss, ab_rs, p_ss, p_rs, f_ss, f_rs, sn_ss, sn_rs, g_ss, g_rs,
    r1_ss, r1_rs, r2_ss, r2_rs, r3_ss, r3_rs,
):
    i = lax.axis_index("gx")
    j = lax.axis_index("gy")
    has_l, has_r = i > 0, i < GX - 1
    has_x = {-1: has_l, 0: True, 1: has_r}
    has_y = {-1: j > 0, 0: True, 1: j < GY - 1}

    def has(d):
        dx, dy = DIRS[d]
        if dx == 0:
            return has_y[dy]
        if dy == 0:
            return has_x[dx]
        return jnp.logical_and(has_x[dx], has_y[dy])

    cy, czh, cc = i // 8, (i // 2) % 4, i % 2
    czl, cx = j // 4, j % 4
    me = cy * 8 + cc * 4 + cx
    mez = czh * 2 + czl
    mine = lax.rem(3 * me, GROUP)

    def member(m):
        return ((m // 8) * 8 + czh * 2 + (m // 4) % 2, czl * 4 + m % 4)

    def zpeer(k):
        return (cy * 8 + (k // 2) * 2 + cc, (k % 2) * 4 + cx)

    loads = [
        pltpu.make_async_copy(a, b, in_s.at[k])
        for k, (a, b) in enumerate(
            (
                (src_h, src), (stf_h, stf), (lev_h, lev), (g_h, g), (w2_h, w2),
                (snp_h, snp), (w1_h, w1),
            )
        )
    ]
    for c in loads:
        c.start()

    bar = pltpu.get_barrier_semaphore()

    def greet(dev):
        pl.semaphore_signal(bar, inc=1, device_id=dev, device_id_type=MESH)

    @pl.loop(1, ZS)
    def _(k):
        greet(zpeer(lax.rem(mez + k, ZS)))

    @pl.loop(1, GROUP)
    def _(k):
        greet(member(lax.rem(me + k, GROUP)))

    @pl.when(has_l)
    def _():
        @pl.loop(0, GY)
        def _(s):
            greet((i - 1, s))

    @pl.when(has_r)
    def _():
        @pl.loop(0, GY)
        def _(s):
            greet((i + 1, s))

    @pl.loop(1, GY)
    def _(k):
        greet((i, lax.rem(j + k, GY)))

    for c in loads[:4]:
        c.wait()
    a_own = 1.0 / (6.0 + stf[...])
    b_own = src[...] * a_own
    A[8:16, 8:16, :] = a_own
    B[8:16, 8:16, :] = b_own
    PP[8:16, 8:16, :] = b_own
    absend[...] = jnp.concatenate([a_own, b_own], axis=1).astype(BF16)
    fysend[0] = lev[:, 0, :]
    fysend[1] = lev[:, 7, :]
    zero_tile = jnp.zeros((T, T, FZ), F32)
    for d, (dx, dy) in enumerate(DIRS):
        xs, ys = pl.ds(8 + 8 * dx, 8), pl.ds(8 + 8 * dy, 8)

        @pl.when(jnp.logical_not(has(d)))
        def _():
            A[xs, ys, :] = zero_tile
            B[xs, ys, :] = zero_tile
            PP[xs, ys, :] = zero_tile

    @pl.when(jnp.logical_not(has_l))
    def _():
        fxr[0] = jnp.zeros((T, FZ), F32)
        snrcv[0] = jnp.zeros((GY, 8, 128), F32)
        grcv[0] = jnp.zeros((16, 4096), BF16)

    @pl.when(jnp.logical_not(has_r))
    def _():
        fxr[1] = jnp.zeros((T, FZ), F32)
        snrcv[2] = jnp.zeros((GY, 8, 128), F32)
        grcv[1] = jnp.zeros((16, 4096), BF16)

    @pl.when(j == 0)
    def _():
        fyr[0] = jnp.zeros((T, FZ), F32)

    @pl.when(j == GY - 1)
    def _():
        fyr[1] = jnp.zeros((T, FZ), F32)

    loads[5].wait()
    snsend[...] = jnp.zeros((8, 8, 128), F32)
    for s in range(1, 8):
        snsend[s, 0:4, 0:64] = snp[order[s]].astype(F32)

    n_bar = (GY - 1) + (GROUP - 1) + (ZS - 1)
    n_bar = n_bar + jnp.where(has_l, GY, 0) + jnp.where(has_r, GY, 0)
    pl.semaphore_wait(bar, n_bar)

    def ab_copy(d, to):
        dx, dy = DIRS[d]
        slot = 7 - d if to else d
        send_dx = dx if to else -dx
        lo, n = tile_rows(-send_dx, RAD if dy == 0 else RAD - 1)
        rows = pl.ds(lo, n)
        return pltpu.make_async_remote_copy(
            src_ref=absend.at[rows], dst_ref=abrcv.at[slot, rows],
            send_sem=ab_ss.at[d], recv_sem=ab_rs.at[slot],
            device_id=(i + dx, j + dy), device_id_type=MESH,
        )

    def p_copy(e, d, to):
        dx, dy = DIRS[d]
        slot = 7 - d if to else d
        lo, n = tile_rows(-dx if to else dx, 8 if dy == 0 else 6)
        rows = pl.ds(lo // 2, n // 2)
        return pltpu.make_async_remote_copy(
            src_ref=psend.at[e, rows], dst_ref=prcv.at[e, slot, rows],
            send_sem=p_ss.at[e, d], recv_sem=p_rs.at[e, slot],
            device_id=(i + dx, j + dy), device_id_type=MESH,
        )

    def fx_copy(side, to):
        slot = 1 - side if to else side
        return pltpu.make_async_remote_copy(
            src_ref=lev.at[0 if side == 0 else 7], dst_ref=fxr.at[slot],
            send_sem=f_ss.at[side], recv_sem=f_rs.at[slot],
            device_id=(i + (2 * side - 1), j), device_id_type=MESH,
        )

    def fy_copy(side, to):
        slot = 1 - side if to else side
        return pltpu.make_async_remote_copy(
            src_ref=fysend.at[side], dst_ref=fyr.at[slot],
            send_sem=f_ss.at[2 + side], recv_sem=f_rs.at[2 + slot],
            device_id=(i, j + (2 * side - 1)), device_id_type=MESH,
        )

    def g_copy(side, to):
        slot = 1 - side if to else side
        return pltpu.make_async_remote_copy(
            src_ref=g.at[side], dst_ref=grcv.at[slot],
            send_sem=g_ss.at[side], recv_sem=g_rs.at[slot],
            device_id=(i + (2 * side - 1), j), device_id_type=MESH,
        )

    def sn_send(d, s):
        return pltpu.make_async_remote_copy(
            src_ref=snsend.at[s], dst_ref=snrcv.at[1 - d, j],
            send_sem=sn_ss.at[d + 1, s], recv_sem=sn_rs.at[1 - d, j],
            device_id=(i + d, s), device_id_type=MESH,
        )

    def sn_recv(d, y):
        return pltpu.make_async_remote_copy(
            src_ref=snsend.at[0], dst_ref=snrcv.at[d + 1, y],
            send_sem=sn_ss.at[d + 1, 0], recv_sem=sn_rs.at[d + 1, y],
            device_id=(i, j), device_id_type=MESH,
        )

    x_sides = ((0, has_l), (1, has_r))
    y_sides = ((0, has_y[-1]), (1, has_y[1]))

    for d in FAR_FIRST:
        pl.when(has(d))(lambda d=d: ab_copy(d, True).start())
    for side, ok in x_sides:
        pl.when(ok)(lambda side=side: fx_copy(side, True).start())
    for side, ok in y_sides:
        pl.when(ok)(lambda side=side: fy_copy(side, True).start())
    def each_snap(lo, hi, act):
        @pl.loop(lo, hi)
        def _(s):
            pl.when(has_l)(lambda: act(-1, s))
            pl.when(s != j)(lambda: act(0, s))
            pl.when(has_r)(lambda: act(1, s))


    loads[4].wait()
    w2p[:, 0:1728] = w2[...].astype(F32)
    even = w2p[...]
    odd = pltpu.roll(even, 64, 1)
    left = iota((64, 128), 1) < 64

    def pair(o):
        t = ((o + 1) // 2) * 128
        return (odd if o % 2 else even)[:, t : t + 128]

    for a in range(3):
        for b in range(3):
            o = 9 * a + 3 * b
            tiles = (
                jnp.where(left, pair(o + 2), 0.0),
                pair(o + 1),
                pair(o),
                jnp.where(left, 0.0, pair(o - 1)),
            )
            for k, v in enumerate(tiles):
                BT[a, 64 * k : 64 * k + 64, 128 * b : 128 * b + 128] = v.astype(BF16)

    loads[6].wait()
    w1s[...] = jnp.zeros((32, 128), F32)
    w1s[0:27, 0:64] = w1[...].astype(F32)
    w1d = w1s[...]
    w1d = jnp.concatenate([w1d, pltpu.roll(w1d, 64, 1)], axis=0).astype(BF16)
    for par in range(2):
        for b in range(3):
            k = iota((256, 64), 0)
            col = iota((256, 64), 1)
            zo = col // 32
            zi = ((k & 63) + 5 - 2 * par) & 3
            cz = zi - zo
            want = 9 * (k // 64) + 3 * b + cz
            hit = (col % 32 == want) & (cz >= 0) & (cz < 3) & (k < 192)
            V[par, :, b * 128 : (b + 1) * 128] = dot(
                jnp.where(hit, 1.0, 0.0).astype(BF16), w1d
            ).astype(BF16)

    lane128 = iota((16, 128), 1)

    def windows(plane, gv):
        gr = pltpu.roll(gv.astype(F32), 64, 1)
        for t in range(33):
            if t == 0:
                tile = jnp.where(lane128 >= 64, gr[:, 0:128], 0.0)
            elif t == 32:
                tile = jnp.where(lane128 < 64, gr[:, 0:128], 0.0)
            else:
                tile = gr[:, 128 * t : 128 * (t + 1)]
            tile = tile.astype(BF16)
            if t < 32:
                r = ((t % 2) * 16 + t // 2) * 16
                W[plane, r : r + 16, 0:128] = tile
            if t > 0:
                r = (((t - 1) % 2) * 16 + (t - 1) // 2) * 16
                W[plane, r : r + 16, 128:256] = tile

    for d in NEAR_FIRST:
        dx, dy = DIRS[d]
        lo, n = tile_rows(dx, RAD if dy == 0 else RAD - 1)
        xs, ys = pl.ds(8 + 8 * dx + lo, n), pl.ds(8 + 8 * dy, 8)

        @pl.when(has(d))
        def _():
            ab_copy(d, False).wait_recv()
            v = abrcv[d, lo : lo + n].astype(F32)
            A[xs, ys, :] = v[:, 0:8]
            B[xs, ys, :] = v[:, 8:16]
            PP[xs, ys, :] = v[:, 8:16]

    def around(v):
        rows = pltpu.roll(v, 1, 0) + pltpu.roll(v, 23, 0)
        return rows + z_before(v, 1) + z_after(v, 1)

    def sweeps(first, count):
        for rad in range(first, first - count, -1):
            lo, hi = 8 - rad, 16 + rad
            before, cur = PP[lo - 1], PP[lo]
            for x in range(lo, hi):
                after = PP[x + 1]
                PP[x] = B[x] + A[x] * (before + after + around(cur))
                before, cur = cur, after

    def exchange(e, filler):
        own = PP[8:16, 8:16, :]
        psend[e] = own.reshape(4, 16, FZ).astype(BF16)
        for d in FAR_FIRST:
            pl.when(has(d))(lambda d=d: p_copy(e, d, True).start())
        filler()
        for d in NEAR_FIRST:
            dx, dy = DIRS[d]
            lo, n = tile_rows(dx, 8 if dy == 0 else 6)
            xs, ys = pl.ds(8 + 8 * dx + lo, n), pl.ds(8 + 8 * dy, 8)

            @pl.when(has(d))
            def _():
                p_copy(e, d, False).wait_recv()
                v = prcv[e, d, lo // 2 : (lo + n) // 2].astype(F32)
                PP[xs, ys, :] = v.reshape(n, 8, FZ)

    def back(x):
        @pl.loop(0, 4)
        def _(q):
            rows = pl.ds(pl.multiple_of(q * 128, 128), 128)
            r = dot(W[x + 2, rows, :], BT[0])
            r = r + dot(W[x + 1, rows, :], BT[1])
            r = r + dot(W[x, rows, :], BT[2])
            dh[x, rows, :] = (
                row_after(r[:, 0:128]) + r[:, 128:256] + row_before(r[:, 256:384])
            )

    lane = iota((64, 128), 1)

    def term(o):
        a, b, c = o // 9, (o // 3) % 3, o % 3
        r = (2 - c) * 64
        cols = slice(b * 128, b * 128 + 128)
        v = jnp.where(lane < 64, acc[a, r : r + 64, cols], acc[a, r + 64 : r + 128, cols])
        return v + pltpu.roll(v, 64, 1)

    def r1_send(m):
        return pltpu.make_async_remote_copy(
            src_ref=rsend.at[m], dst_ref=r1.at[me],
            send_sem=r1_ss.at[m], recv_sem=r1_rs.at[me],
            device_id=member(lax.rem(11 * m, GROUP)), device_id_type=MESH,
        )

    def r1_recv(m):
        return pltpu.make_async_remote_copy(
            src_ref=rsend.at[0], dst_ref=r1.at[m],
            send_sem=r1_ss.at[0], recv_sem=r1_rs.at[m],
            device_id=member(m), device_id_type=MESH,
        )

    def r2_copy(k, slot):
        return pltpu.make_async_remote_copy(
            src_ref=r2.at[mez], dst_ref=r2.at[slot],
            send_sem=r2_ss.at[k], recv_sem=r2_rs.at[slot],
            device_id=zpeer(k), device_id_type=MESH,
        )

    def r3_copy(m, slot):
        return pltpu.make_async_remote_copy(
            src_ref=f3, dst_ref=r3.at[slot],
            send_sem=r3_ss.at[m], recv_sem=r3_rs.at[slot],
            device_id=member(m), device_id_type=MESH,
        )

    def first_gradient():
        spread = jnp.where((iota((16, ROWS), 1) & 15) == iota((16, ROWS), 0), 1.0, 0.0).astype(BF16)
        r_k = iota((256, ROWS), 0) & 63
        r_c = iota((256, ROWS), 1)
        jj = 2 * ((r_c & 255) // 16) + r_c // 256
        t = r_k - 2 * jj + 1
        near = (t >= 0) & (t < 4)
        for x in range(2):
            LT[x] = jnp.where(near, dot(CC[x + 1].T.astype(BF16), spread), 0.0).astype(BF16)
        parts = []
        for par in range(2):
            cols = slice(par * 256, par * 256 + 256)
            q = dot(LT[0, :, cols], DZ3[0, cols, :]) + dot(LT[1, :, cols], DZ3[1, cols, :])
            q = q.reshape(4, 8, 8, 384)
            parts.append([q[a].sum(0) for a in range(3)])
        d1[...] = jnp.zeros((64, 128), F32)
        for a in range(3):
            u, w = parts[0][a], parts[1][a]
            u = u + pltpu.roll(u, 4, 0)
            w = w + pltpu.roll(w, 4, 0)
            u = u + pltpu.roll(w, 2, 0)
            for b in range(3):
                v = u[:, b * 128 : (b + 1) * 128]
                v = pltpu.roll(v, 64, 1) + pltpu.roll(v, 7, 0)
                v = pltpu.roll(v, 1, 0)
                d1[9 * a + 3 * b : 9 * a + 3 * b + 3, :] = v[0:3]

    def layers():
        snrcv[1, j] = snsend[j]
        @pl.when(has_l)
        def _():
            @pl.loop(0, GY)
            def _(y):
                sn_recv(-1, y).wait_recv()

        @pl.when(has_r)
        def _():
            @pl.loop(0, GY)
            def _(y):
                sn_recv(1, y).wait_recv()

        @pl.loop(1, GY)
        def _(k):
            sn_recv(0, lax.rem(j + k, GY)).wait_recv()

        for d in range(3):
            for y in range(8):
                t = snrcv[d, y]
                S6[2 * d, 2 * y : 2 * y + 2, :] = t[0:2]
                S6[2 * d + 1, 2 * y : 2 * y + 2, :] = t[2:4]
        for p in range(4):
            CC[p, :, 0:128] = S6[p] + pltpu.roll(S6[p + 1], 64, 1)
            CC[p, :, 128:256] = S6[p + 2]

        for p in range(4):
            keep = {0: jnp.where(has_l, 1.0, 0.0), 3: jnp.where(has_r, 1.0, 0.0)}.get(p)

            for q in range(4):
                rows = slice(q * 128, q * 128 + 128)
                par = q // 2
                jj = 2 * ((q % 2) * 8 + iota((8, 16, 256), 0)) + par
                t = (iota((8, 16, 256), 2) & 63) - 2 * jj + 1
                mask = (t >= 0) & (t < 4)
                v = jnp.broadcast_to(CC[p][None], (8, 16, 256))
                v = jnp.where(mask, v, 0.0).reshape(128, 256).astype(BF16)
                r = dot(v, V[par])
                z = row_before(r[:, 0:128]) + r[:, 128:256] + row_after(r[:, 256:384])
                sig = 1.0 / (1.0 + jnp.exp(-z))
                h = z * sig
                if keep is not None:
                    h = h * keep
                H3[p, rows, 0:128] = row_before(h).astype(BF16)
                H3[p, rows, 128:256] = h.astype(BF16)
                H3[p, rows, 256:384] = row_after(h).astype(BF16)
                if p in (1, 2):
                    dz = dh[p - 1, rows, :] * (sig * (1.0 + z * (1.0 - sig)))
                    DZ3[p - 1, rows, 0:128] = row_after(dz).astype(BF16)
                    DZ3[p - 1, rows, 128:256] = dz.astype(BF16)
                    DZ3[p - 1, rows, 256:384] = row_before(dz).astype(BF16)

        for a in range(3):
            acc[a] = dot(GT[0], H3[a]) + dot(GT[1], H3[a + 1])
            if a == 2:
                first_gradient()
            for q in range((0, 4, 9)[a], (4, 9, 14)[a]):
                other = term(2 * q + 1) if q < 13 else d1[...]
                v = jnp.where(lane < 64, term(2 * q), other)
                rsend[2 * q] = v[0:32].astype(BF16)
                rsend[2 * q + 1] = v[32:64].astype(BF16)
            c0, n = (0, 8, 18)[a], (8, 10, 10)[a]

            @pl.loop(0, n)
            def _(k):
                m = c0 + lax.rem(me + k, n)
                pl.when(m != mine)(lambda: r1_send(m).start())

    def filler_one():
        each_snap(1, GY, lambda d, s: sn_send(d, s).start())
        for side, ok in x_sides:
            pl.when(ok)(lambda side=side: g_copy(side, True).start())
        for x in range(2):
            windows(x + 1, g[x])
            GT[x] = W[x + 1].T

    def filler_two():
        for side, ok in x_sides:
            pl.when(ok)(lambda side=side: g_copy(side, False).wait_recv())
        windows(0, grcv[0])
        windows(3, grcv[1])
        back(0)
        back(1)

    sweeps(RAD - 1, RAD)
    exchange(0, filler_one)
    sweeps(6, 7)
    exchange(1, filler_two)
    sweeps(6, 6)

    for side, ok in x_sides:
        pl.when(ok)(lambda side=side: fx_copy(side, False).wait_recv())
    for side, ok in y_sides:
        pl.when(ok)(lambda side=side: fy_copy(side, False).wait_recv())

    pool = jnp.where(iota((FZ, 128), 0) // 4 == iota((FZ, 128), 1), 1.0 / 64.0, 0.0).astype(BF16)
    row8 = iota((8, FZ), 0)
    sums = []
    total = None
    for x in range(8):
        pc = PP[x + 8]
        px = 0.5 * (PP[x + 9, 8:16] - PP[x + 7, 8:16])
        py = 0.5 * (pltpu.roll(pc, 23, 0) - pltpu.roll(pc, 1, 0))[8:16]
        pm = pc[8:16]
        pz = 0.5 * (z_after(pm, 1) - z_before(pm, 1))
        fm = lev[x]
        f_lo = fxr[0] if x == 0 else lev[x - 1]
        f_hi = fxr[1] if x == 7 else lev[x + 1]
        fx = 0.5 * (f_hi - f_lo)
        y_lo = jnp.where(row8 == 0, fyr[0, x : x + 1, :], pltpu.roll(fm, 1, 0))
        y_hi = jnp.where(row8 == 7, fyr[1, x : x + 1, :], pltpu.roll(fm, 7, 0))
        fy = 0.5 * (y_hi - y_lo)
        fz = 0.5 * (z_after(fm, 1) - z_before(fm, 1))
        new = fm + 2.0 * (px * fx + py * fy + pz * fz)
        newl[x] = new
        prs[x] = pm
        total = new if x % 4 == 0 else total + new
        if x % 4 == 3:
            t = total + pltpu.roll(total, 7, 0)
            sums.append(t + pltpu.roll(t, 6, 0))
    rest, mean = jnp.concatenate(sums, axis=0), 0.0
    for _ in range(3):
        part = rest.astype(BF16)
        rest = rest - part.astype(F32)
        mean = mean + dot(part, pool)
    for r in range(4):
        snsend[0, r : r + 1, :] = mean[4 * r : 4 * r + 1, :]
    snsend[0, 4:8, :] = jnp.zeros((4, 128), F32)

    each_snap(0, 1, lambda d, s: sn_send(d, s).start())
    stores = [
        pltpu.make_async_copy(a, b, out_s.at[k])
        for k, (a, b) in enumerate(
            ((newl, newl_h), (prs, prs_h), (r3, sum_h))
        )
    ]
    stores[0].start()
    stores[1].start()
    layers()

    for d in range(8):
        @pl.when(has(d))
        def _():
            ab_copy(d, True).wait_send()
            p_copy(0, d, True).wait_send()
            p_copy(1, d, True).wait_send()

    for side, ok in x_sides:
        @pl.when(ok)
        def _():
            fx_copy(side, True).wait_send()
            g_copy(side, True).wait_send()

    for side, ok in y_sides:
        pl.when(ok)(lambda side=side: fy_copy(side, True).wait_send())
    each_snap(0, GY, lambda d, s: sn_send(d, s).wait_send())

    @pl.when(mine < CHUNKS)
    def _():
        def add(k, total):
            m = lax.rem(me + k, GROUP)
            r1_recv(m).wait_recv()
            return total + r1[m].astype(F32)

        r2[mez] = lax.fori_loop(1, GROUP, add, rsend[mine].astype(F32))

        for k in (4, 3, 5, 2, 6, 1, 7):
            r2_copy(lax.rem(mez + k, ZS), mez).start()
        for k in (7, 1, 6, 2, 5, 3, 4):
            m = lax.rem(mez + k, ZS)
            r2_copy(m, m).wait_recv()

        total = r2[0]
        for k in range(1, ZS):
            total = total + r2[k]
        f3[...] = total.astype(BF16)

        for dy, dx in sorted(
            ((y, x) for y in range(4) for x in range(4)),
            key=lambda v: -min(v[0], 4 - v[0]) - min(v[1], 4 - v[1]),
        ):
            for dc in range(2):
                if (dy, dx, dc) != (0, 0, 0):
                    y, x, c = lax.rem(cy + dy, 4), lax.rem(cx + dx, 4), lax.rem(cc + dc, 2)
                    r3_copy(y * 8 + c * 4 + x, mine).start()

        r3[mine] = f3[...]

    @pl.loop(0, CHUNKS)
    def _(m):
        pl.when(m != mine)(lambda: r1_send(m).wait_send())

    @pl.when(mine < CHUNKS)
    def _():
        @pl.loop(1, ZS)
        def _(k):
            r2_copy(lax.rem(mez + k, ZS), mez).wait_send()

    @pl.loop(0, CHUNKS)
    def _(m):
        pl.when(m != mine)(lambda: r3_copy(m, m).wait_recv())

    stores[2].start()

    @pl.when(mine < CHUNKS)
    def _():
        @pl.loop(1, GROUP)
        def _(k):
            r3_copy(lax.rem(me + k, GROUP), mine).wait_send()

    for c in stores:
        c.wait()


def leave(
    newl_h, prs_h, sum_h, newl_o, prs_o, dw1_o, dw2_o,
    newl, prs, total, dw1, dw2, in_s, out_s,
):
    ins = [
        pltpu.make_async_copy(a, b, in_s.at[k])
        for k, (a, b) in enumerate(((sum_h, total), (newl_h, newl), (prs_h, prs)))
    ]
    outs = [
        pltpu.make_async_copy(a, b, out_s.at[k])
        for k, (a, b) in enumerate(
            ((newl, newl_o), (prs, prs_o), (dw1, dw1_o), (dw2, dw2_o))
        )
    ]
    for c in ins:
        c.start()
    ins[0].wait()
    for q in range(14):
        v = jnp.concatenate([total[2 * q], total[2 * q + 1]], axis=0).astype(F32)
        if q < 13:
            dw2[:, 128 * q : 128 * q + 128] = v
        else:
            dw2[:, 128 * q : 128 * q + 64] = v[:, 0:64]
            dw1[...] = pltpu.roll(v, 64, 1)[0:27, 0:64]
    outs[3].start()
    outs[2].start()
    ins[1].wait()
    outs[0].start()
    ins[2].wait()
    outs[1].start()
    for c in outs:
        c.wait()


def per_device(
    level_set, source, stiffness, snap_buffer, buffer_order, first_weight, second_weight, out_grad
):
    snap = snap_buffer.reshape(8, 4, 64)
    g = out_grad.reshape(2, 16, 4096)
    sm = pl.BlockSpec(memory_space=pltpu.SMEM)
    hbm = pl.BlockSpec(memory_space=pltpu.HBM)
    dma = pltpu.SemaphoreType.DMA
    shapes = (
        jax.ShapeDtypeStruct((8, 8, FZ), F32),
        jax.ShapeDtypeStruct((8, 8, FZ), F32),
        jax.ShapeDtypeStruct((27, 64), F32),
        jax.ShapeDtypeStruct((64, 1728), F32),
    )
    sums = jax.ShapeDtypeStruct((CHUNKS, 32, 128), BF16)
    results = pl.pallas_call(
        kernel,
        out_shape=shapes[:2] + (sums,),
        in_specs=[hbm, hbm, hbm, hbm, sm, hbm, hbm, hbm],
        out_specs=(hbm,) * 3,
        scratch_shapes=[
            pltpu.VMEM((8, 8, FZ), F32),
            pltpu.VMEM((8, 8, FZ), F32),
            dma((3,)),
            pltpu.VMEM((8, 8, FZ), F32),
            pltpu.VMEM((8, 8, FZ), F32),
            pltpu.VMEM((8, 8, FZ), F32),
            pltpu.VMEM((64, 1728), BF16),
            pltpu.VMEM((2, 16, 4096), BF16),
            pltpu.VMEM((8, 4, 64), BF16),
            pltpu.VMEM((27, 64), BF16),
            pltpu.VMEM((64, 1792), F32),
            dma((7,)),
            pltpu.VMEM((24, 24, FZ), F32),
            pltpu.VMEM((24, 24, FZ), F32),
            pltpu.VMEM((24, 24, FZ), F32),
            pltpu.VMEM((8, 16, FZ), BF16),
            pltpu.VMEM((8, 8, 16, FZ), BF16),
            pltpu.VMEM((2, 4, 16, FZ), BF16),
            pltpu.VMEM((2, 8, 4, 16, FZ), BF16),
            pltpu.VMEM((2, 8, FZ), F32),
            pltpu.VMEM((2, 8, FZ), F32),
            pltpu.VMEM((2, 8, FZ), F32),
            pltpu.VMEM((8, 8, 128), F32),
            pltpu.VMEM((3, 8, 8, 128), F32),
            pltpu.VMEM((2, 16, 4096), BF16),
            pltpu.VMEM((4, ROWS, 256), BF16),
            pltpu.VMEM((2, 256, ROWS), BF16),
            pltpu.VMEM((3, 256, 384), BF16),
            pltpu.VMEM((2, 256, 384), BF16),
            pltpu.VMEM((32, 128), F32),
            pltpu.VMEM((6, 16, 128), F32),
            pltpu.VMEM((4, 16, 256), F32),
            pltpu.VMEM((4, ROWS, 384), BF16),
            pltpu.VMEM((2, ROWS, 384), BF16),
            pltpu.VMEM((2, 256, ROWS), BF16),
            pltpu.VMEM((2, ROWS, 128), F32),
            pltpu.VMEM((3, 256, 384), F32),
            pltpu.VMEM((64, 128), F32),
            pltpu.VMEM((CHUNKS, 32, 128), BF16),
            pltpu.VMEM((GROUP, 32, 128), BF16),
            pltpu.VMEM((ZS, 32, 128), F32),
            pltpu.VMEM((32, 128), BF16),
            pltpu.VMEM((CHUNKS, 32, 128), BF16),
            dma((8,)), dma((8,)), dma((2, 8)), dma((2, 8)), dma((4,)), dma((4,)),
            dma((3, 8)), dma((3, 8)), dma((2,)), dma((2,)),
            dma((CHUNKS,)), dma((GROUP,)), dma((ZS,)), dma((ZS,)), dma((GROUP,)), dma((CHUNKS,)),
        ],
        compiler_params=pltpu.CompilerParams(
            collective_id=0, has_side_effects=True, vmem_limit_bytes=60 * 1024 * 1024
        ),
    )(source, stiffness, level_set, snap, buffer_order, first_weight, second_weight.T, g)
    results = pl.pallas_call(
        leave,
        out_shape=shapes,
        in_specs=[hbm] * 3,
        out_specs=(hbm,) * 4,
        scratch_shapes=[
            pltpu.VMEM(shapes[0].shape, F32),
            pltpu.VMEM(shapes[1].shape, F32),
            pltpu.VMEM(sums.shape, BF16),
            pltpu.VMEM(shapes[2].shape, F32),
            pltpu.VMEM(shapes[3].shape, F32),
            dma((3,)),
            dma((4,)),
        ],
        compiler_params=pltpu.CompilerParams(vmem_limit_bytes=60 * 1024 * 1024),
    )(*results)
    return results[0], results[1], results[2], results[3].T


def solution(mesh):
    placed = (
        P("gx", "gy", None),
        P("gx", "gy", None),
        P("gx", "gy", None),
        P(None, "gx", "gy", None),
        P(),
        P(),
        P(),
        P("gy", "gx", None, None),
    )
    return jax.shard_map(
        per_device,
        mesh=mesh,
        in_specs=placed,
        out_specs=(P("gx", "gy", None), P("gx", "gy", None), P(), P()),
        check_vma=False,
    )
```
